128 devices in a mesh: section: 2 (over z_hi), shard: 2 (over core), replica: 32 (over x, y, z_lo).
Axes of the slice: x: 4, y: 4, z: 4 (z_hi: 2, z_lo: 2; z = z_hi * 2 + z_lo), core: 2. Of those that a mesh axis runs over, the one named last changes fastest.
Arguments:
- tokens: bfloat16 [2, 8192, 576], P(None, ('shard', 'replica')), may hold values from -6 to 6
- cotangent: bfloat16 [2, 8192, 576], P(None, ('shard', 'replica')), may hold values from -6 to 6
- seq_lengths: int32 [2, 128], P(None, ('shard', 'replica')), may hold values from 0 to 128, as said below
- gain_attn: bfloat16 [2, 576], P('section', 'shard'), may hold values from 0.5 to 1.5
- w_query: bfloat16 [2, 576, 576], P('section', 'shard'), may hold values from -0.25 to 0.25
- w_key: bfloat16 [2, 576, 192], P('section', 'shard'), may hold values from -0.25 to 0.25
- w_value: bfloat16 [2, 576, 192], P('section', 'shard'), may hold values from -0.25 to 0.25
- w_out: bfloat16 [2, 576, 576], P('section', 'shard'), may hold values from -1 to 1
- gain_ffn: bfloat16 [2, 576], P('section', 'shard'), may hold values from 0.5 to 1.5
- w_gate: bfloat16 [2, 576, 1536], P('section', 'shard'), may hold values from -0.25 to 0.25
- w_up: bfloat16 [2, 576, 1536], P('section', 'shard'), may hold values from -0.25 to 0.25
- w_down: bfloat16 [2, 1536, 576], P('section', 'shard'), may hold values from -0.21875 to 0.21875
Outputs:
- activations: bfloat16 [2, 2, 8192, 576], P('section', None, ('shard', 'replica'))
- input_grads: bfloat16 [2, 2, 8192, 576], P('section', None, ('shard', 'replica'))
- grad_gain_attn: float32 [2, 576], P('section', 'shard')
- grad_query: float32 [2, 576, 576], P('section', 'shard')
- grad_key: float32 [2, 576, 192], P('section', 'shard')
- grad_value: float32 [2, 576, 192], P('section', 'shard')
- grad_out: float32 [2, 576, 576], P('section', 'shard')
- grad_gain_ffn: float32 [2, 576], P('section', 'shard')
- grad_gate: float32 [2, 576, 1536], P('section', 'shard')
- grad_up: float32 [2, 576, 1536], P('section', 'shard')
- grad_down: float32 [2, 1536, 576], P('section', 'shard')
The draws below stay inside these ranges and needn't reach their ends.
Inputs may be any that keep to these rules, and one draw needn't show every extreme that they name: `seq_lengths`: the 2 lengths of one token group's micro-batch sum to at most 128; in every micro-batch one token group holds a single sequence of 128.
All inputs are finite; a program needn't handle non-finite values.
Results may differ from the reference program's by a relative error of at most 0.03.
Values may be sent and summed in bfloat16 or wider, within the bound.
A program may use at most 128 MiB of HBM per device.

```python
import math
import jax
import jax.numpy as jnp
from jax import lax

D = 576
H = 9
KV = 3
HD = 64
FF = 1536
ROWS = 128
MICRO = 2
SEQS = 2
LAYERS = 2
GROUPS = 64
TOKENS = 8192


def draw_seq_lengths(key, part):
    key = jax.random.fold_in(key, 7)
    first_key, second_key, third_key = jax.random.split(key, 3)
    leading = jax.random.randint(first_key, (MICRO, GROUPS), ROWS // 2, ROWS + 1, dtype=jnp.int32)
    spare = (ROWS - leading).astype(jnp.int32)
    fraction = jax.random.randint(second_key, (MICRO, GROUPS), 0, 1024, dtype=jnp.int32)
    trailing = (spare * fraction // 1023).astype(jnp.int32)
    chosen = jax.random.randint(third_key, (MICRO, 1), 0, GROUPS, dtype=jnp.int32)
    filled = jnp.arange(GROUPS, dtype=jnp.int32)[None, :] == chosen
    leading = jnp.where(filled, ROWS, leading).astype(jnp.int32)
    trailing = jnp.where(filled, 0, trailing).astype(jnp.int32)
    others = jnp.zeros((MICRO, GROUPS, SEQS - 2), jnp.int32)
    lengths = jnp.concatenate([leading[..., None], trailing[..., None], others], -1)
    return lengths.reshape(MICRO, GROUPS * SEQS).astype(jnp.int32)


def shard_levels(stream_key, shape, cuts, smallest, top_value):
    gain = 1.0
    for dim, shards_of in cuts:
        draws = jax.random.uniform(jax.random.fold_in(jax.random.fold_in(stream_key, 6), dim), (shards_of,), jnp.float32, smallest / len(cuts), top_value / len(cuts))
        gain = gain * jnp.repeat(jnp.exp(draws), shape[dim] // shards_of).reshape((-1,) + (1,) * (len(shape) - 1 - dim))
    return gain


def gaussian(key, shape, deviation, bound, shards=(), kind=jnp.bfloat16):
    drawn = deviation * jax.random.normal(key, shape, jnp.float32)
    if shards:
        drawn = drawn * shard_levels(key, shape, shards, -0.22, 0.18)
    return jnp.clip(drawn, -bound, bound).astype(kind)


def setup_inputs(seed: int = 0) -> dict:
    arg_keys = jax.random.split(jax.random.key(seed), 13)
    tokens = gaussian(arg_keys[0], (MICRO, TOKENS, D), 1.0, 6.0, ((1, 64),))
    cotangent = gaussian(arg_keys[1], (MICRO, TOKENS, D), 1.0, 6.0, ((1, 64),))
    seq_lengths = draw_seq_lengths(jax.random.fold_in(arg_keys[12], 71), 0)
    gain_attn = jnp.clip(1.0 + 0.1 * jax.random.normal(arg_keys[3], (LAYERS, D), jnp.float32), 0.5, 1.5).astype(jnp.bfloat16)
    w_query = gaussian(arg_keys[4], (LAYERS, D, H * HD), D ** -0.5, 0.25, ((0, 2), (1, 2)))
    w_key = gaussian(arg_keys[5], (LAYERS, D, KV * HD), D ** -0.5, 0.25, ((0, 2), (1, 2)))
    w_value = gaussian(arg_keys[6], (LAYERS, D, KV * HD), D ** -0.5, 0.25, ((0, 2), (1, 2)))
    w_out = gaussian(arg_keys[7], (LAYERS, H * HD, D), (max(H * HD // 16, 8)) ** -0.5, 1.0, ((0, 2), (1, 2)))
    gain_ffn = jnp.clip(1.0 + 0.1 * jax.random.normal(arg_keys[8], (LAYERS, D), jnp.float32), 0.5, 1.5).astype(jnp.bfloat16)
    w_gate = gaussian(arg_keys[9], (LAYERS, D, FF), D ** -0.5, 0.25, ((0, 2), (1, 2)))
    w_up = gaussian(arg_keys[10], (LAYERS, D, FF), D ** -0.5, 0.25, ((0, 2), (1, 2)))
    w_down = gaussian(arg_keys[11], (LAYERS, FF, D), (FF // 2) ** -0.5, 0.21875, ((0, 2), (1, 2)))
    return dict(tokens=tokens, cotangent=cotangent, seq_lengths=seq_lengths, gain_attn=gain_attn, w_query=w_query, w_key=w_key, w_value=w_value, w_out=w_out, gain_ffn=gain_ffn, w_gate=w_gate, w_up=w_up, w_down=w_down)


@jax.custom_vjp
def low(v):
    return lax.optimization_barrier(v.astype(jnp.bfloat16)).astype(jnp.float32)

@jax.custom_vjp
def low_back(v):
    return v

def low_keep(v):
    return (low(v), None)

def low_pass(kept, grad):
    return (grad,)

def back_keep(v):
    return (v, None)

def back_low(kept, grad):
    return (low(grad),)
low.defvjp(low_keep, low_pass)
low_back.defvjp(back_keep, back_low)
highest = lax.Precision.HIGHEST
eps_norm = 1e-05
rope_base = 100000.0

def matmul(left, right):
    return jnp.dot(left, right, precision=highest, preferred_element_type=jnp.float32)

def layout(lengths):
    row_ids = jnp.arange(ROWS, dtype=jnp.int32)
    seq_ends = jnp.cumsum(lengths, axis=-1).astype(jnp.int32)
    passed = (row_ids[:, None] >= seq_ends[..., None, :]).astype(jnp.int32)
    segment = lax.optimization_barrier(jnp.sum(passed, axis=-1)).astype(jnp.int32)
    starts = lax.optimization_barrier(jnp.sum(passed * lengths[..., None, :], axis=-1)).astype(jnp.int32)
    position = (row_ids - starts).astype(jnp.int32)
    live_rows = (row_ids < seq_ends[..., -1:]).astype(jnp.float32)
    return (segment, position, live_rows)

def rope_tables(position):
    half_dim = HD // 2
    freq_idx = jnp.arange(half_dim, dtype=jnp.float32)
    inverse = jnp.exp(freq_idx * (-2.0 * math.log(rope_base) / HD))
    angles = position.astype(jnp.float32)[:, None] * inverse[None, :]
    cosine = jnp.cos(angles)
    sine_val = jnp.sin(angles)
    return (jnp.concatenate([cosine, cosine], -1), jnp.concatenate([sine_val, sine_val], -1))

def rotate(values, cosine, sine_val):
    half_dim = values.shape[-1] // 2
    turned = jnp.concatenate([-values[..., half_dim:], values[..., :half_dim]], -1)
    return values * cosine[:, None, :] + turned * sine_val[:, None, :]

def block(hidden_in, params, segment, position):
    gain_one, w_query, w_key, w_value, w_out, gain_two, w_gate, w_up, w_down = params
    row_count = hidden_in.shape[0]
    normed = hidden_in * lax.rsqrt(lax.optimization_barrier(jnp.mean(hidden_in * hidden_in, axis=-1, keepdims=True)) + eps_norm)
    entry = low(normed * gain_one)
    query = low_back(matmul(entry, w_query)).reshape(row_count, H, HD)
    keys_raw = low_back(matmul(entry, w_key)).reshape(row_count, KV, HD)
    values_b = low(low_back(matmul(entry, w_value))).reshape(row_count, KV, HD)
    cosine, sine_val = rope_tables(position)
    query_rot = low(rotate(query, cosine, sine_val)).reshape(row_count, KV, H // KV, HD)
    key_rot = low(rotate(keys_raw, cosine, sine_val))
    scores = low_back(jnp.einsum('rkgd,ckd->kgrc', query_rot, key_rot, precision=highest)) * HD ** (-0.5)
    row_ids = jnp.arange(row_count)
    allowed = (segment[:, None] == segment[None, :]) & (row_ids[None, :] <= row_ids[:, None])
    scores = jnp.where(allowed, scores, -1e+30)
    probs = low(jax.nn.softmax(scores, axis=-1))
    mixed = low(low_back(jnp.einsum('kgrc,ckd->rkgd', probs, values_b, precision=highest)))
    mixed = mixed.reshape(row_count, H * HD)
    middle = hidden_in + low_back(matmul(mixed, w_out))
    normed_two = middle * lax.rsqrt(lax.optimization_barrier(jnp.mean(middle * middle, axis=-1, keepdims=True)) + eps_norm)
    second = low(normed_two * gain_two)
    gate_val = low_back(matmul(second, w_gate))
    up_val = low_back(matmul(second, w_up))
    inner = low(jax.nn.silu(gate_val) * up_val)
    return middle + low_back(matmul(inner, w_down))

def reference(tokens, cotangent, seq_lengths, gain_attn, w_query, w_key, w_value, w_out, gain_ffn, w_gate, w_up, w_down):
    blocks = MICRO * GROUPS
    lengths = seq_lengths.reshape(blocks, SEQS)
    segment, position, live_rows = layout(lengths)
    inputs = tokens.astype(jnp.float32).reshape(blocks, ROWS, D)
    upstream = cotangent.astype(jnp.float32).reshape(blocks, ROWS, D) * live_rows[..., None]
    params = tuple((p.astype(jnp.float32) for p in (gain_attn, w_query, w_key, w_value, w_out, gain_ffn, w_gate, w_up, w_down)))
    shifts = jnp.zeros((LAYERS, blocks, ROWS, D), jnp.float32)

    def forward(inputs, params, shifts):
        outputs = []
        hidden_in = low_back(inputs + shifts[0])
        result = inputs
        for layer in range(LAYERS):
            weights = tuple((p[layer] for p in params))
            result = jax.vmap(block, in_axes=(0, None, 0, 0))(hidden_in, weights, segment, position)
            outputs.append(result)
            if layer + 1 < LAYERS:
                hidden_in = low_back(low(result) + shifts[layer + 1])
        return (result, outputs)
    result, pullback, outputs = jax.vjp(forward, inputs, params, shifts, has_aux=True)
    grad_inputs, grads, grad_shifts = pullback(upstream)
    activations = jnp.stack([o.astype(jnp.bfloat16) for o in outputs]).reshape(LAYERS, MICRO, TOKENS, D)
    input_grads = grad_shifts.astype(jnp.bfloat16).reshape(LAYERS, MICRO, TOKENS, D)
    return (activations, input_grads, grads[0], grads[1], grads[2], grads[3], grads[4], grads[5], grads[6], grads[7], grads[8])
```

```python
import functools
import math

import jax
import jax.numpy as jnp
from jax import lax
from jax.experimental import pallas as pl
from jax.experimental.pallas import tpu as pltpu
from jax.sharding import PartitionSpec as P

MESH = pl.DeviceIdType.MESH
F32 = jnp.float32
BF16 = jnp.bfloat16

D = 576
HD = 64
FF = 1536
ROWS = 128
MICRO = 2
M = MICRO * ROWS
OWN = D // 2
EPS = 1e-05
BASE = 100000.0
VMEM_LIMIT = 56 * 1024 * 1024

GATE = 0
UP = GATE + 12 * OWN
DOWN = UP + 12 * OWN
QKV = DOWN + 6 * D
OUT = QKV + 8 * OWN
GAIN = OUT + 4 * OWN
USED = GAIN + OWN
FLAT = 14336
HALF = FLAT // 2
P1 = HALF // 4
P2 = P1 // 4
P3 = P2 // 2


def dot(a, b):
    return lax.dot_general(a, b, (((1,), (0,)), ((), ())), preferred_element_type=F32)


def dot_nt(a, b):
    return lax.dot_general(a, b, (((1,), (1,)), ((), ())), preferred_element_type=F32)


def dot_tn(a, b):
    return lax.dot_general(a, b, (((0,), (0,)), ((), ())), preferred_element_type=F32)


def lanes():
    return lax.broadcasted_iota(jnp.int32, (ROWS, 128), 1)


def slots():
    return lax.broadcasted_iota(jnp.int32, (ROWS, 128), 0)


def ends(lens, m):
    return lens[m, 0], lens[m, 0] + lens[m, 1]


def segment_of(ids, first_end, last_end):
    return jnp.where(ids >= first_end, 1, 0) + jnp.where(ids >= last_end, 1, 0)


def tables(lens, cs, sn):
    lane = lanes()
    inverse = jnp.exp((lane % 32).astype(F32) * (-2.0 * math.log(BASE) / HD))
    for m in range(MICRO):
        first_end, last_end = ends(lens, m)
        r = slots()
        position = r - jnp.where(r >= first_end, lens[m, 0], 0)
        position = position - jnp.where(r >= last_end, lens[m, 1], 0)
        angle = position.astype(F32) * inverse
        sine = jnp.sin(angle)
        cs[m] = jnp.cos(angle)
        sn[m] = jnp.where(lane % 64 < 32, -sine, sine)


def turned(u, lane):
    return jnp.where(lane % 64 < 32, pltpu.roll(u, 96, 1), pltpu.roll(u, 32, 1))


def both_halves(u, half, lane):
    return jnp.where(lane // 64 == half, u, pltpu.roll(u, 64, 1))


def norm_scale(x):
    return lax.rsqrt(jnp.mean(x * x, axis=-1, keepdims=True) + EPS)


def gains_of(wq):
    turned_gains = wq[:, 896:1024].astype(F32).T
    return turned_gains[64:65], turned_gains[65:66]


def norm_back(upper, normed, scale):
    return scale * (upper - normed * jnp.mean(upper * normed, axis=-1, keepdims=True))


def attention_forward(x, lens, wq, wo, g1, s):
    entry = (x * norm_scale(x) * g1).astype(BF16)
    s["ent"][...] = entry
    qkv = dot(entry, wq[...])
    lane = lanes()
    for m in range(MICRO):
        rows = slice(m * ROWS, (m + 1) * ROWS)
        cosine, sine = s["cs"][m], s["sn"][m]
        first_end, last_end = ends(lens, m)
        allowed = (
            segment_of(slots(), first_end, last_end) == segment_of(lane, first_end, last_end)
        ) & (lane <= slots())
        allowed = jnp.concatenate([allowed.astype(F32)] * 3, axis=0) > 0.5
        blocks = []
        for b in range(6):
            u = qkv[rows, 128 * b : 128 * b + 128]
            blocks.append(u * cosine + turned(u, lane) * sine)
        heads = []
        for kv in range(3):
            i = m * 3 + kv
            kj = 9 + kv
            key = both_halves(blocks[kj // 2], kj % 2, lane).astype(BF16)
            vb = qkv[rows, 768 + 128 * (kv // 2) : 896 + 128 * (kv // 2)]
            value = both_halves(vb, kv % 2, lane).astype(BF16)
            query = jnp.concatenate(
                [
                    jnp.where(lane // 64 == j % 2, blocks[j // 2], 0.0).astype(BF16)
                    for j in range(3 * kv, 3 * kv + 3)
                ],
                axis=0,
            )
            s["kd"][i] = key
            s["vd"][i] = value
            s["qs"][i] = query
            scores = jnp.where(allowed, dot_nt(query, key) * HD**-0.5, -1e30)
            weights = jnp.exp(scores - jnp.max(scores, axis=-1, keepdims=True))
            probs = weights / jnp.sum(weights, axis=-1, keepdims=True)
            s["pr"][i] = probs
            out = dot(probs.astype(BF16), value)
            heads += [out[ROWS * g : ROWS * (g + 1)] for g in range(3)]
        for b in range(4):
            s["mix"][rows, 128 * b : 128 * b + 128] = jnp.where(
                lane < 64, heads[2 * b], heads[2 * b + 1]
            ).astype(BF16)
        s["mix"][rows, 512:576] = heads[8][:, :64].astype(BF16)
    middle = x + dot(s["mix"][...], wo[...])
    s["mid"][...] = middle
    return middle


def feed_forward(middle, g2, wg, wu, wd, s, keep):
    second = (middle * norm_scale(middle) * g2).astype(BF16)
    s["sec"][...] = second
    for j in range(0, FF, 256):
        cols = slice(j, j + 256)
        gate = dot(second, wg[:, cols])
        up = dot(second, wu[:, cols])
        sig = 1.0 / (1.0 + jnp.exp(-gate))
        swish = gate * sig
        s["inn"][:, cols] = (swish * up).astype(BF16)
        if keep:
            s["fa"][:, cols] = up * sig * (1.0 + gate * (1.0 - sig))
            s["fb"][:, cols] = swish
    return middle + dot(s["inn"][...], wd[...])


def backward_inputs(x, dy, wq, wo, g1, g2, wg, wu, wd, s, t):
    middle = s["mid"][...]
    scale_two = norm_scale(middle)
    n2 = middle * scale_two
    df = dy.astype(BF16)
    t["df"][...] = df
    for j in range(0, FF, 256):
        cols = slice(j, j + 256)
        d_inner = dot_nt(df, wd[cols, :])
        t["dg"][:, cols] = (d_inner * s["fa"][:, cols]).astype(BF16)
        t["du"][:, cols] = (d_inner * s["fb"][:, cols]).astype(BF16)
    d_second = dot_nt(t["dg"][...], wg[...]) + dot_nt(t["du"][...], wu[...])
    gain_two = jnp.sum(d_second * n2, axis=0, keepdims=True)
    d_middle = dy + norm_back(d_second * g2, n2, scale_two)
    branch = d_middle.astype(BF16)
    t["db"][...] = branch
    d_mixed = dot_nt(branch, wo[...])
    lane = lanes()
    for m in range(MICRO):
        rows = slice(m * ROWS, (m + 1) * ROWS)
        cosine, sine = s["cs"][m], s["sn"][m]
        dq, dk, dv = [], [], []
        for kv in range(3):
            i = m * 3 + kv
            parts = []
            for j in range(3 * kv, 3 * kv + 3):
                if j < 8:
                    block = d_mixed[rows, 128 * (j // 2) : 128 * (j // 2) + 128]
                    block = jnp.where(lane // 64 == j % 2, block, 0.0)
                else:
                    block = jnp.concatenate(
                        [d_mixed[rows, 512:576], jnp.zeros((ROWS, 64), F32)], axis=1
                    )
                parts.append(block.astype(BF16))
            upper = jnp.concatenate(parts, axis=0)
            probs = s["pr"][i]
            d_probs = dot_nt(upper, s["vd"][i])
            value = dot_tn(probs.astype(BF16), upper)
            dv.append(value + pltpu.roll(value, 64, 1))
            total = jnp.sum(d_probs * probs, axis=-1, keepdims=True)
            d_scores = (probs * (d_probs - total) * HD**-0.5).astype(BF16)
            query = dot(d_scores, s["kd"][i])
            dq += [query[ROWS * g : ROWS * (g + 1)] for g in range(3)]
            key = dot_tn(d_scores, s["qs"][i])
            dk.append(key + pltpu.roll(key, 64, 1))
        heads = dq + dk
        for b in range(6):
            u = jnp.where(lane < 64, heads[2 * b], heads[2 * b + 1])
            t["dqkv"][rows, 128 * b : 128 * b + 128] = (
                u * cosine - turned(u, lane) * sine
            ).astype(BF16)
        t["dqkv"][rows, 768:896] = jnp.where(lane < 64, dv[0], dv[1]).astype(BF16)
        t["dqkv"][rows, 896:1024] = jnp.where(lane < 64, dv[2], 0.0).astype(BF16)
    d_entry = dot_nt(t["dqkv"][...], wq[...])
    scale_one = norm_scale(x)
    n1 = x * scale_one
    gain_one = jnp.sum(d_entry * n1, axis=0, keepdims=True)
    dx = d_middle + norm_back(d_entry * g1, n1, scale_one)
    return dx, d_middle, gain_one, gain_two


def flat_store(flat, start, block, count):
    flat[0, start : start + count] = block[:count].astype(BF16)
    flat[1, start : start + count] = block[count:].astype(BF16)


def weight_grads(d_middle, gain_one, gain_two, s, t, flat):
    second_t = s["sec"][...].T
    for b in range(0, 12, 2):
        for key, start in (("dg", GATE), ("du", UP)):
            g = dot(second_t, t[key][:, 128 * b : 128 * b + 256])
            flat_store(flat, start + b * OWN, g[:, :128], OWN)
            flat_store(flat, start + (b + 1) * OWN, g[:, 128:], OWN)
    df_t = t["df"][...].T
    for b in range(0, 12, 2):
        g = dot(df_t, s["inn"][:, 128 * b : 128 * b + 256]).astype(BF16)
        owner, first = b // 6, DOWN + (b % 6) * D
        flat[owner, first : first + D] = g[:, :128]
        flat[owner, first + D : first + 2 * D] = g[:, 128:]
    entry_t = s["ent"][...].T
    mixed_t = s["mix"][...].T
    for b in range(0, 6, 2):
        g = dot(entry_t, t["dqkv"][:, 128 * b : 128 * b + 256])
        flat_store(flat, QKV + b * OWN, g[:, :128], OWN)
        flat_store(flat, QKV + (b + 1) * OWN, g[:, 128:], OWN)
    g = dot(entry_t, t["dqkv"][:, 768:1024])
    flat_store(flat, QKV + 6 * OWN, g[:, :128], OWN)
    rest = jnp.concatenate([d_middle[:, 512:576], jnp.zeros((M, 64), F32)], axis=1)
    rest = pltpu.roll(rest, 64, 1).astype(BF16)
    flat_store(flat, QKV + 7 * OWN, g[:, 128:] + dot(mixed_t, rest), OWN)
    for b in range(0, 4, 2):
        g = dot(mixed_t, t["db"][:, 128 * b : 128 * b + 256])
        flat_store(flat, OUT + b * OWN, g[:, :128], OWN)
        flat_store(flat, OUT + (b + 1) * OWN, g[:, 128:], OWN)
    row = lax.broadcasted_iota(jnp.int32, (128, D), 0)
    gains = jnp.where(row == 0, gain_one, jnp.where(row == 1, gain_two, 0.0)).T
    flat_store(flat, GAIN, gains, OWN)
    flat[0, USED:] = jnp.zeros((FLAT - USED, 128), BF16)
    flat[1, USED:] = jnp.zeros((FLAT - USED, 128), BF16)


SAVED = {
    "ent": ((M, D), BF16),
    "qs": ((6, 3 * ROWS, 128), BF16),
    "kd": ((6, ROWS, 128), BF16),
    "vd": ((6, ROWS, 128), BF16),
    "pr": ((6, 3 * ROWS, 128), F32),
    "mix": ((M, D), BF16),
    "mid": ((M, D), F32),
    "sec": ((M, D), BF16),
    "inn": ((M, FF), BF16),
    "fa": ((M, FF), F32),
    "fb": ((M, FF), F32),
    "cs": ((MICRO, ROWS, 128), F32),
    "sn": ((MICRO, ROWS, 128), F32),
}
TEMPS = {
    "df": ((M, D), BF16),
    "dg": ((M, FF), BF16),
    "du": ((M, FF), BF16),
    "db": ((M, D), BF16),
    "dqkv": ((M, 1024), BF16),
}


def scratch(table, names=None):
    return [pltpu.VMEM(*table[k]) for k in (names or table)]


def rows_of(ref):
    return jnp.concatenate([ref[0], ref[1]], axis=0).astype(F32)


def store_rows(ref, value):
    for m in range(MICRO):
        ref[m] = value[m * ROWS : (m + 1) * ROWS].astype(BF16)


def forward_kernel(lens, x_ref, wq, wo, wg, wu, wd, y_ref, *saved):
    s = dict(zip(SAVED, saved))
    g1, g2 = gains_of(wq)
    tables(lens, s["cs"], s["sn"])
    middle = attention_forward(rows_of(x_ref), lens, wq, wo, g1, s)
    store_rows(y_ref, feed_forward(middle, g2, wg, wu, wd, s, False))


def middle_kernel(lens, x_ref, cot, wq, wo, wg, wu, wd, y_ref, dx_ref, *refs):
    s = dict(zip(SAVED, refs))
    t = dict(zip(TEMPS, refs[len(SAVED) :]))
    g1, g2 = gains_of(wq)
    tables(lens, s["cs"], s["sn"])
    x = rows_of(x_ref)
    middle = attention_forward(x, lens, wq, wo, g1, s)
    store_rows(y_ref, feed_forward(middle, g2, wg, wu, wd, s, True))
    dy = live_rows(cot, lens)
    dx = backward_inputs(x, dy, wq, wo, g1, g2, wg, wu, wd, s, t)[0]
    store_rows(dx_ref, dx)


def live_rows(cot, lens):
    ids = lax.broadcasted_iota(jnp.int32, (ROWS, D), 0)
    return jnp.concatenate(
        [jnp.where(ids < ends(lens, m)[1], cot[m].astype(F32), 0.0) for m in range(MICRO)], axis=0
    )


def last_kernel(lens, x_ref, cot, received, wq, wo, wg, wu, wd, *refs):
    s = dict(zip(SAVED, refs))
    dx_ref, flat = refs[len(SAVED) : len(SAVED) + 2]
    t = dict(zip(TEMPS, refs[len(SAVED) + 2 :]))
    g1, g2 = gains_of(wq)
    x = rows_of(x_ref)
    first = lax.axis_index("section") == 0
    dy = jnp.where(first, rows_of(received), live_rows(cot, lens))
    dx, d_middle, gain_one, gain_two = backward_inputs(x, dy, wq, wo, g1, g2, wg, wu, wd, s, t)
    store_rows(dx_ref, dx)
    weight_grads(d_middle, gain_one, gain_two, s, t, flat)


def vmem(n):
    return [pl.BlockSpec(memory_space=pltpu.VMEM)] * n


def smem():
    return [pl.BlockSpec(memory_space=pltpu.SMEM)]


def shapes(table):
    return [jax.ShapeDtypeStruct(*v) for v in table.values()]


def params(**kw):
    return pltpu.CompilerParams(vmem_limit_bytes=VMEM_LIMIT, **kw)


ROW_SHAPE = jax.ShapeDtypeStruct((MICRO, ROWS, D), BF16)


def run_forward(lens, x, weights):
    return pl.pallas_call(
        forward_kernel,
        out_shape=ROW_SHAPE,
        in_specs=smem() + vmem(6),
        out_specs=vmem(1)[0],
        scratch_shapes=scratch(SAVED),
        compiler_params=params(),
    )(lens, x, *weights)


def run_middle(lens, x, cot, weights):
    out = pl.pallas_call(
        middle_kernel,
        out_shape=[ROW_SHAPE, ROW_SHAPE] + shapes(SAVED),
        in_specs=smem() + vmem(7),
        out_specs=vmem(2 + len(SAVED)),
        scratch_shapes=scratch(TEMPS),
        compiler_params=params(),
    )(lens, x, cot, *weights)
    return out[0], out[1], out[2:]


def run_last(lens, x, cot, received, weights, saved):
    return pl.pallas_call(
        last_kernel,
        out_shape=[ROW_SHAPE, jax.ShapeDtypeStruct((2, FLAT, 128), BF16)],
        in_specs=smem() + vmem(8 + len(SAVED)),
        out_specs=vmem(2),
        scratch_shapes=scratch(TEMPS),
        compiler_params=params(),
    )(lens, x, cot, received, *weights, *saved)


def gather_kernel(*refs):
    ins, outs = refs[:5], refs[5:10]
    send, recv, local = refs[10:]
    section, core, replica = (lax.axis_index(a) for a in ("section", "shard", "replica"))
    other = (section, 1 - core, replica)
    barrier = pltpu.get_barrier_semaphore()
    pl.semaphore_signal(barrier, inc=1, device_id=other, device_id_type=MESH)
    pl.semaphore_wait(barrier, 1)
    copies = []
    for i, (src, dst) in enumerate(zip(ins, outs)):
        count = src.shape[0]
        place = dst.at[pl.ds(pl.multiple_of(core * count, 16), count)]
        copies.append(
            pltpu.make_async_remote_copy(
                src, place, send.at[i], recv.at[i], device_id=other, device_id_type=MESH
            )
        )
        copies.append(pltpu.make_async_copy(src, place, local.at[i]))
    for copy in copies:
        copy.start()
    for copy in copies:
        copy.wait()


def run_gather(parts):
    return pl.pallas_call(
        gather_kernel,
        out_shape=[jax.ShapeDtypeStruct((2 * p.shape[0], p.shape[1]), p.dtype) for p in parts],
        in_specs=[pl.BlockSpec(memory_space=pl.ANY)] * 5,
        out_specs=vmem(5),
        scratch_shapes=[pltpu.SemaphoreType.DMA((5,))] * 3,
        compiler_params=params(collective_id=1, has_side_effects=True),
    )(*parts)


def sum_kernel(g, o, st, rc, one, two, zr, cs_, cr, cl, s1, r1, s2, r2, sz, rz, sg, rg, sh, rh):
    section, core, replica = (lax.axis_index(a) for a in ("section", "shard", "replica"))
    x, y, z = replica // 8, replica // 2 % 4, replica % 2

    def at(x_, y_, z_):
        return (section, core, x_ * 8 + y_ * 2 + z_)

    x_next, x_prev = at((x + 1) % 4, y, z), at((x + 3) % 4, y, z)
    y_next, y_prev = at(x, (y + 1) % 4, z), at(x, (y + 3) % 4, z)
    z_pair = at(x, y, 1 - z)
    partner = (section, 1 - core, replica)
    first_pos, second_pos = (x, y), (y, x)
    first_dev = ((x_next, x_prev), (y_next, y_prev))
    second_dev = ((y_next, y_prev), (x_next, x_prev))

    barrier = pltpu.get_barrier_semaphore()
    for device in (partner, x_next, x_prev, y_next, y_prev, z_pair):
        pl.semaphore_signal(barrier, inc=1, device_id=device, device_id_type=MESH)
    pl.semaphore_wait(barrier, 6)

    sent = []

    def send(src, dst, send_sem, recv_sem, device):
        copy = pltpu.make_async_remote_copy(
            src, dst, send_sem, recv_sem, device_id=device, device_id_type=MESH
        )
        copy.start()
        sent.append(copy)
        return copy

    def span(start, count):
        return pl.ds(pl.multiple_of(start, 16), count)

    def wide(ref, index):
        return ref[index].astype(F32)

    cross, own = {}, {}
    for k in (2, 1, 3, 0):
        for h in range(2):
            rows = span(HALF * h + P1 * ((first_pos[h] + k) % 4), P1)
            i = h * 4 + k
            cross[h, k] = send(g.at[1 - core, rows], rc.at[i], cs_.at[i], cr.at[i], partner)
            own[h, k] = pltpu.make_async_copy(g.at[core, rows], st.at[i], cl.at[i])
            own[h, k].start()

    def ring(h, buf, sems, recvs, devs, src, n):
        up, down = devs
        half = n // 2

        def go(i, ref, device):
            return send(ref, buf.at[h * 6 + i], sems.at[h * 6 + i], recvs.at[h * 6 + i], device)

        return go, up, down, half

    h1 = P1 // 2
    first = {}
    for k in (2, 1, 3):
        for h in range(2):
            go, up, down, _ = ring(h, one, s1, r1, first_dev[h], None, P1)
            cross[h, k].wait_recv()
            own[h, k].wait()
            i = h * 4 + k
            st[i] = (wide(st, i) + wide(rc, i)).astype(BF16)
            if k == 2:
                first[h, 0] = go(0, st.at[i, :h1], up)
                first[h, 1] = go(1, st.at[i, h1:], down)
            elif k == 1:
                first[h, 2] = go(2, st.at[i, h1:], up)
            else:
                first[h, 3] = go(3, st.at[i, :h1], down)
    for h in range(2):
        go, up, down, _ = ring(h, one, s1, r1, first_dev[h], None, P1)
        first[h, 0].wait_recv()
        st[h * 4 + 1, :h1] = (st[h * 4 + 1, :h1].astype(F32) + wide(one, h * 6)).astype(BF16)
        first[h, 4] = go(4, st.at[h * 4 + 1, :h1], up)
        first[h, 1].wait_recv()
        st[h * 4 + 3, h1:] = (st[h * 4 + 3, h1:].astype(F32) + wide(one, h * 6 + 1)).astype(BF16)
        first[h, 5] = go(5, st.at[h * 4 + 3, h1:], down)

    h2 = P2 // 2
    second = {}

    def piece(h, k):
        return P2 * ((second_pos[h] + k) % 4)

    for h in range(2):
        cross[h, 0].wait_recv()
        own[h, 0].wait()
        i = h * 4
        first[h, 3].wait_recv()
        first[h, 4].wait_recv()
        st[i, :h1] = (
            st[i, :h1].astype(F32)
            + rc[i, :h1].astype(F32)
            + wide(one, h * 6 + 3)
            + wide(one, h * 6 + 4)
        ).astype(BF16)
        first[h, 2].wait_recv()
        first[h, 5].wait_recv()
        st[i, h1:] = (
            st[i, h1:].astype(F32)
            + rc[i, h1:].astype(F32)
            + wide(one, h * 6 + 2)
            + wide(one, h * 6 + 5)
        ).astype(BF16)
        go, up, down, _ = ring(h, two, s2, r2, second_dev[h], None, P2)
        second[h, 0] = go(0, st.at[i, span(piece(h, 2), h2)], up)
        second[h, 1] = go(1, st.at[i, span(piece(h, 2) + h2, h2)], down)
        second[h, 2] = go(2, st.at[i, span(piece(h, 1) + h2, h2)], up)
        second[h, 3] = go(3, st.at[i, span(piece(h, 3), h2)], down)
    for h in range(2):
        go, up, down, _ = ring(h, two, s2, r2, second_dev[h], None, P2)
        i = h * 4
        second[h, 0].wait_recv()
        rows = span(piece(h, 1), h2)
        st[i, rows] = (st[i, rows].astype(F32) + wide(two, h * 6)).astype(BF16)
        second[h, 4] = go(4, st.at[i, rows], up)
        second[h, 1].wait_recv()
        rows = span(piece(h, 3) + h2, h2)
        st[i, rows] = (st[i, rows].astype(F32) + wide(two, h * 6 + 1)).astype(BF16)
        second[h, 5] = go(5, st.at[i, rows], down)
    zed = {}
    for h in range(2):
        i = h * 4
        rows = span(piece(h, 0), h2)
        second[h, 3].wait_recv()
        second[h, 4].wait_recv()
        st[i, rows] = (
            st[i, rows].astype(F32) + wide(two, h * 6 + 3) + wide(two, h * 6 + 4)
        ).astype(BF16)
        rows = span(piece(h, 0) + h2, h2)
        second[h, 2].wait_recv()
        second[h, 5].wait_recv()
        st[i, rows] = (
            st[i, rows].astype(F32) + wide(two, h * 6 + 2) + wide(two, h * 6 + 5)
        ).astype(BF16)
        zed[h] = send(
            st.at[i, span(piece(h, 0) + P3 * (1 - z), P3)], zr.at[h], sz.at[h], rz.at[h], z_pair
        )

    def block(h, k1, k2, part=None):
        start = HALF * h + P1 * ((first_pos[h] + k1) % 4) + piece(h, k2)
        if part is None:
            return o.at[span(start, P2)]
        return o.at[span(start + P3 * ((z + part) % 2), P3)]

    def give(ref, sems, recvs, i, device):
        return send(ref, ref, sems.at[i], recvs.at[i], device)

    back, along = {}, {}
    for h in range(2):
        zed[h].wait_recv()
        here = piece(h, 0) + P3 * z
        start = HALF * h + P1 * first_pos[h] + here
        o[span(start, P3)] = (
            st[h * 4, span(here, P3)].astype(F32) + wide(zr, h)
        ).astype(BF16)
        ref = block(h, 0, 0, 0)
        zed[h] = give(ref, sz, rz, 2 + h, z_pair)
        for d in range(2):
            along[h, d, 0] = give(ref, sg, rg, h * 6 + d * 3, second_dev[h][d])
    for h in range(2):
        zed[h].wait_recv()
        ref = block(h, 0, 0, 1)
        for d in range(2):
            along[h, d, 1] = give(ref, sg, rg, h * 6 + d * 3 + 1, second_dev[h][d])
        for d in range(2):
            back[h, d, 0] = give(block(h, 0, 0), sh, rh, h * 12 + d * 6, first_dev[h][d])
    for h in range(2):
        along[h, 0, 0].wait_recv()
        along[h, 0, 2] = give(block(h, 0, 3, 0), sg, rg, h * 6 + 2, second_dev[h][0])
        along[h, 1, 0].wait_recv()
        along[h, 1, 1].wait_recv()
        along[h, 1, 2] = give(block(h, 0, 1, 1), sg, rg, h * 6 + 5, second_dev[h][1])
        for d in range(2):
            back[h, d, 1] = give(block(h, 0, 1), sh, rh, h * 12 + d * 6 + 1, first_dev[h][d])
        along[h, 0, 1].wait_recv()
        for d in range(2):
            back[h, d, 3] = give(block(h, 0, 3), sh, rh, h * 12 + d * 6 + 3, first_dev[h][d])
    for h in range(2):
        along[h, 0, 2].wait_recv()
        along[h, 1, 2].wait_recv()
        for d in range(2):
            back[h, d, 2] = give(block(h, 0, 2), sh, rh, h * 12 + d * 6 + 2, first_dev[h][d])
    ahead = {}
    for k in (0, 1, 3, 2):
        for h in range(2):
            back[h, 0, k].wait_recv()
            back[h, 1, k].wait_recv()
            if k in (0, 3):
                ahead[h, k] = give(
                    block(h, 3, k), sh, rh, h * 12 + 4 + (k == 3), first_dev[h][0]
                )
            else:
                ahead[h, k] = give(
                    block(h, 1, k), sh, rh, h * 12 + 10 + (k == 2), first_dev[h][1]
                )
    for copy in ahead.values():
        copy.wait_recv()
    for copy in sent:
        copy.wait_send()


def run_sum(flat):
    dma = pltpu.SemaphoreType.DMA
    return pl.pallas_call(
        sum_kernel,
        out_shape=jax.ShapeDtypeStruct((FLAT, 128), BF16),
        in_specs=[pl.BlockSpec(memory_space=pl.ANY)],
        out_specs=vmem(1)[0],
        scratch_shapes=[
            pltpu.VMEM((8, P1, 128), BF16),
            pltpu.VMEM((8, P1, 128), BF16),
            pltpu.VMEM((12, P1 // 2, 128), BF16),
            pltpu.VMEM((12, P2 // 2, 128), BF16),
            pltpu.VMEM((2, P3, 128), BF16),
            dma((8,)),
            dma((8,)),
            dma((8,)),
            dma((12,)),
            dma((12,)),
            dma((12,)),
            dma((12,)),
            dma((4,)),
            dma((4,)),
            dma((12,)),
            dma((12,)),
            dma((24,)),
            dma((24,)),
        ],
        compiler_params=params(collective_id=2, has_side_effects=True),
    )(flat)


def unpack_kernel(f, gain_one, wq, wk, wv, wo, gain_two, wg, wu, wd):
    def rows(start, count=OWN):
        return f[start : start + count].astype(F32)

    for b in range(12):
        cols = slice(128 * b, 128 * b + 128)
        wg[0, :, cols] = rows(GATE + b * OWN)
        wu[0, :, cols] = rows(UP + b * OWN)
    for b in range(6):
        wd[0, 128 * b : 128 * b + 128, :] = rows(DOWN + b * D, D).T
    for b in range(4):
        wq[0, :, 128 * b : 128 * b + 128] = rows(QKV + b * OWN)
        wo[0, :, 128 * b : 128 * b + 128] = rows(OUT + b * OWN)
    swap = [pltpu.roll(rows(QKV + b * OWN), 64, 1) for b in range(4, 8)]
    wq[0, :, 512:576] = rows(QKV + 4 * OWN)[:, :64]
    lane = lax.broadcasted_iota(jnp.int32, (OWN, 128), 1)
    wk[0, :, :128] = jnp.where(lane < 64, swap[0], swap[1])
    wk[0, :, 128:] = swap[1][:, :64]
    wv[0, :, :128] = rows(QKV + 6 * OWN)
    wv[0, :, 128:] = rows(QKV + 7 * OWN)[:, :64]
    wo[0, :, 512:576] = swap[3][:, :64]
    gains = rows(GAIN).T
    gain_one[...] = gains[0:1]
    gain_two[...] = gains[1:2]


def run_unpack(flat):
    kinds = [(1, OWN), (1, OWN, D), (1, OWN, 192), (1, OWN, 192), (1, OWN, D)]
    kinds += [(1, OWN), (1, OWN, FF), (1, OWN, FF), (1, FF // 2, D)]
    return pl.pallas_call(
        unpack_kernel,
        out_shape=[jax.ShapeDtypeStruct(k, F32) for k in kinds],
        in_specs=vmem(1),
        out_specs=vmem(9),
        compiler_params=params(),
    )(flat)


def over(value, by):
    return lax.ppermute(value, "section", [(0, 1)] if by > 0 else [(1, 0)])


def shards(
    tokens,
    cotangent,
    seq_lengths,
    gain_attn,
    w_query,
    w_key,
    w_value,
    w_out,
    gain_ffn,
    w_gate,
    w_up,
    w_down,
):
    first = lax.axis_index("section") == 0
    side = jnp.concatenate(
        [
            w_query[0],
            w_key[0],
            w_value[0],
            gain_attn[0][:, None],
            gain_ffn[0][:, None],
            jnp.zeros((OWN, 62), BF16),
        ],
        axis=1,
    )
    weights = run_gather([side, w_out[0], w_gate[0], w_up[0], w_down[0]])
    early = run_forward(seq_lengths, tokens, weights)
    layer_in = jnp.where(first, tokens, over(early, 1))
    result, d_early, saved = run_middle(seq_lengths, layer_in, cotangent, weights)
    received = over(d_early, -1)
    d_input, flat = run_last(seq_lengths, layer_in, cotangent, received, weights, saved)
    grads = run_unpack(run_sum(flat))
    return (result[None], d_input[None], *grads)


def solution(mesh):
    row_spec = P(None, ("shard", "replica"), None)
    out_spec = P("section", None, ("shard", "replica"), None)
    vector = P("section", "shard")
    matrix = P("section", "shard", None)
    weight_specs = (vector, matrix, matrix, matrix, matrix, vector, matrix, matrix, matrix)
    return jax.shard_map(
        shards,
        mesh=mesh,
        in_specs=(row_spec, row_spec, P(None, ("shard", "replica")), *weight_specs),
        out_specs=(out_spec, out_spec, *weight_specs),
        check_vma=False,
    )
```

```python
import functools
import math

import jax
import jax.numpy as jnp
from jax import lax
from jax.experimental import pallas as pl
from jax.experimental.pallas import tpu as pltpu
from jax.sharding import PartitionSpec as P

MESH = pl.DeviceIdType.MESH
F32 = jnp.float32
BF16 = jnp.bfloat16

D = 576
HD = 64
FF = 1536
ROWS = 128
MICRO = 2
M = MICRO * ROWS
OWN = D // 2
EPS = 1e-05
BASE = 100000.0
VMEM_LIMIT = 62 * 1024 * 1024

GATE = 0
UP = GATE + 12 * OWN
DOWN = UP + 12 * OWN
QKV = DOWN + 6 * D
OUT = QKV + 8 * OWN
GAIN = OUT + 4 * OWN
USED = GAIN + OWN
FLAT = 14336
HALF = FLAT // 2
P1 = HALF // 4
P2 = P1 // 4
P3 = P2 // 2


def dot(a, b):
    return lax.dot_general(a, b, (((1,), (0,)), ((), ())), preferred_element_type=F32)


def dot_nt(a, b):
    return lax.dot_general(a, b, (((1,), (1,)), ((), ())), preferred_element_type=F32)


def dot_tn(a, b):
    return lax.dot_general(a, b, (((0,), (0,)), ((), ())), preferred_element_type=F32)


def lanes():
    return lax.broadcasted_iota(jnp.int32, (ROWS, 128), 1)


def slots():
    return lax.broadcasted_iota(jnp.int32, (ROWS, 128), 0)


def segment_of(ids, first_end, last_end):
    return jnp.where(ids >= first_end, 1, 0) + jnp.where(ids >= last_end, 1, 0)


def turned(u, lane):
    return jnp.where(lane % 64 < 32, pltpu.roll(u, 96, 1), pltpu.roll(u, 32, 1))


def both_halves(u, half, lane):
    return jnp.where(lane // 64 == half, u, pltpu.roll(u, 64, 1))


def norm_scale(x):
    return lax.rsqrt(jnp.mean(x * x, axis=-1, keepdims=True) + EPS)


def norm_back(upper, normed, scale):
    return scale * (upper - normed * jnp.mean(upper * normed, axis=-1, keepdims=True))


def lengths_of(r, m):
    first = r["lens"][m, 0:1, 0:1].astype(jnp.int32)
    return first, first + r["lens"][m, 0:1, 1:2].astype(jnp.int32)


def tables(r, m):
    first_end, last_end = lengths_of(r, m)
    lane, slot = lanes(), slots()
    inverse = jnp.exp((lane % 32).astype(F32) * (-2.0 * math.log(BASE) / HD))
    position = slot - jnp.where(slot >= first_end, first_end, 0)
    position = position - jnp.where(slot >= last_end, last_end - first_end, 0)
    angle = position.astype(F32) * inverse
    sine = jnp.sin(angle)
    r["cs"][m] = jnp.cos(angle)
    r["sn"][m] = jnp.where(lane % 64 < 32, -sine, sine)


def side_rows(wq, wk, wv, gain_one, gain_two):
    lane = lax.broadcasted_iota(jnp.int32, (OWN, 128), 1)
    none = jnp.zeros((OWN, 64), F32)
    tail = jnp.concatenate([wq[:, 512:576].astype(F32), none], axis=1)
    key_a = pltpu.roll(wk[:, :128].astype(F32), 64, 1)
    key_b = pltpu.roll(jnp.concatenate([wk[:, 128:192].astype(F32), none], axis=1), 64, 1)
    last = jnp.concatenate([wv[:, 128:192].astype(F32), none], axis=1)
    row = lax.broadcasted_iota(jnp.int32, (128, OWN), 0)
    gains = jnp.where(
        row == 64, gain_one[...].astype(F32), jnp.where(row == 65, gain_two[...].astype(F32), 0.0)
    ).T
    return {
        512: jnp.where(lane < 64, tail, key_a),
        640: jnp.where(lane < 64, key_a, key_b),
        768: wv[:, :128].astype(F32),
        896: last + gains,
    }


def forward(r, m, arrived):
    tables(r, m)
    x = r["x"][m]
    arrived("side")
    wq, wo, wg, wu, wd = (r[k] for k in ("wq", "wo", "wg", "wu", "wd"))
    gains = wq[:, 896:1024].astype(F32).T
    g1, g2 = gains[64:65], gains[65:66]
    entry = (x * norm_scale(x) * g1).astype(BF16)
    r["ent"][m] = entry
    qkv = dot(entry, wq[...])
    lane = lanes()
    cosine, sine = r["cs"][m], r["sn"][m]
    first_end, last_end = lengths_of(r, m)
    allowed = (
        segment_of(slots(), first_end, last_end) == segment_of(lane, first_end, last_end)
    ) & (lane <= slots())
    allowed = jnp.concatenate([allowed.astype(F32)] * 3, axis=0) > 0.5
    blocks = []
    for b in range(6):
        u = qkv[:, 128 * b : 128 * b + 128]
        blocks.append(u * cosine + turned(u, lane) * sine)
    heads = []
    for kv in range(3):
        kj = 9 + kv
        key = both_halves(blocks[kj // 2], kj % 2, lane).astype(BF16)
        vb = qkv[:, 768 + 128 * (kv // 2) : 896 + 128 * (kv // 2)]
        value = both_halves(vb, kv % 2, lane).astype(BF16)
        query = jnp.concatenate(
            [
                jnp.where(lane // 64 == j % 2, blocks[j // 2], 0.0).astype(BF16)
                for j in range(3 * kv, 3 * kv + 3)
            ],
            axis=0,
        )
        r["kd"][m, kv] = key
        r["vd"][m, kv] = value
        r["qs"][m, kv] = query
        scores = jnp.where(allowed, dot_nt(query, key) * HD**-0.5, -1e30)
        weights = jnp.exp(scores - jnp.max(scores, axis=-1, keepdims=True))
        probs = weights / jnp.sum(weights, axis=-1, keepdims=True)
        r["pr"][m, kv] = probs
        out = dot(probs.astype(BF16), value)
        heads += [out[ROWS * g : ROWS * (g + 1)] for g in range(3)]
    for b in range(4):
        r["mix"][m, :, 128 * b : 128 * b + 128] = jnp.where(
            lane < 64, heads[2 * b], heads[2 * b + 1]
        ).astype(BF16)
    r["mix"][m, :, 512:576] = heads[8][:, :64].astype(BF16)
    arrived("wo")
    middle = x + dot(r["mix"][m], wo[...])
    r["mid"][m] = middle
    second = (middle * norm_scale(middle) * g2).astype(BF16)
    r["sec"][m] = second
    arrived("wg")
    arrived("wu")
    for j in range(0, FF, 256):
        cols = slice(j, j + 256)
        gate = dot(second, wg[:, cols])
        up = dot(second, wu[:, cols])
        sig = 1.0 / (1.0 + jnp.exp(-gate))
        swish = gate * sig
        r["inn"][m, :, cols] = (swish * up).astype(BF16)
        r["fa"][m, :, cols] = up * sig * (1.0 + gate * (1.0 - sig))
        r["fb"][m, :, cols] = swish
    arrived("wd")
    return middle + dot_nt(r["inn"][m], wd[...])


def backward(r, m):
    wq, wo, wg, wu, wd = (r[k] for k in ("wq", "wo", "wg", "wu", "wd"))
    gains = wq[:, 896:1024].astype(F32).T
    g1, g2 = gains[64:65], gains[65:66]
    dy = r["dy"][m]
    middle = r["mid"][m]
    scale_two = norm_scale(middle)
    n2 = middle * scale_two
    df = dy.astype(BF16)
    r["df"][m] = df
    for j in range(0, FF, 256):
        cols = slice(j, j + 256)
        d_inner = dot(df, wd[:, cols])
        r["dg"][m, :, cols] = (d_inner * r["fa"][m, :, cols]).astype(BF16)
        r["du"][m, :, cols] = (d_inner * r["fb"][m, :, cols]).astype(BF16)
    d_second = dot_nt(r["dg"][m], wg[...]) + dot_nt(r["du"][m], wu[...])
    r["gsum"][m, 1:2, :] = jnp.sum(d_second * n2, axis=0, keepdims=True)
    d_middle = dy + norm_back(d_second * g2, n2, scale_two)
    branch = d_middle.astype(BF16)
    r["db"][m] = branch
    d_mixed = dot_nt(branch, wo[...])
    lane = lanes()
    cosine, sine = r["cs"][m], r["sn"][m]
    dq, dk, dv = [], [], []
    for kv in range(3):
        parts = []
        for j in range(3 * kv, 3 * kv + 3):
            if j < 8:
                block = d_mixed[:, 128 * (j // 2) : 128 * (j // 2) + 128]
                block = jnp.where(lane // 64 == j % 2, block, 0.0)
            else:
                block = jnp.concatenate([d_mixed[:, 512:576], jnp.zeros((ROWS, 64), F32)], axis=1)
            parts.append(block.astype(BF16))
        upper = jnp.concatenate(parts, axis=0)
        probs = r["pr"][m, kv]
        d_probs = dot_nt(upper, r["vd"][m, kv])
        value = dot_tn(probs.astype(BF16), upper)
        dv.append(value + pltpu.roll(value, 64, 1))
        total = jnp.sum(d_probs * probs, axis=-1, keepdims=True)
        d_scores = (probs * (d_probs - total) * HD**-0.5).astype(BF16)
        query = dot(d_scores, r["kd"][m, kv])
        dq += [query[ROWS * g : ROWS * (g + 1)] for g in range(3)]
        key = dot_tn(d_scores, r["qs"][m, kv])
        dk.append(key + pltpu.roll(key, 64, 1))
    heads = dq + dk
    for b in range(6):
        u = jnp.where(lane < 64, heads[2 * b], heads[2 * b + 1])
        r["dqkv"][m, :, 128 * b : 128 * b + 128] = (u * cosine - turned(u, lane) * sine).astype(
            BF16
        )
    r["dqkv"][m, :, 768:896] = jnp.where(lane < 64, dv[0], dv[1]).astype(BF16)
    r["dqkv"][m, :, 896:1024] = jnp.where(lane < 64, dv[2], 0.0).astype(BF16)
    d_entry = dot_nt(r["dqkv"][m], wq[...])
    x = r["x"][m]
    scale_one = norm_scale(x)
    n1 = x * scale_one
    r["gsum"][m, 0:1, :] = jnp.sum(d_entry * n1, axis=0, keepdims=True)
    return d_middle + norm_back(d_entry * g1, n1, scale_one)


def weight_grads(r, flat, done):
    def whole(name, cols=slice(None)):
        value = r[name][:, :, cols]
        return value.reshape(M, value.shape[-1])

    def store(start, block):
        flat[0, start : start + OWN] = block[:OWN].astype(BF16)
        flat[1, start : start + OWN] = block[OWN:].astype(BF16)
        done(start + OWN)

    second_t = whole("sec").T
    for name, start in (("dg", GATE), ("du", UP)):
        for b in range(0, 12, 2):
            g = dot(second_t, whole(name, slice(128 * b, 128 * b + 256)))
            store(start + b * OWN, g[:, :128])
            store(start + (b + 1) * OWN, g[:, 128:])
    df_t = whole("df").T
    for b in range(6):
        for owner in range(2):
            g = dot(df_t, whole("inn", slice(768 * owner + 128 * b, 768 * owner + 128 * b + 128)))
            flat[owner, DOWN + b * D : DOWN + (b + 1) * D] = g.astype(BF16)
        done(DOWN + (b + 1) * D)
    entry_t = whole("ent").T
    mixed_t = whole("mix").T
    for b in range(0, 8, 2):
        g = dot(entry_t, whole("dqkv", slice(128 * b, 128 * b + 256)))
        store(QKV + b * OWN, g[:, :128])
        if b == 6:
            rest = whole("db", slice(512, 576)).astype(F32)
            rest = jnp.concatenate([rest, jnp.zeros((M, 64), F32)], axis=1)
            rest = pltpu.roll(rest, 64, 1).astype(BF16)
            store(QKV + 7 * OWN, g[:, 128:] + dot(mixed_t, rest))
        else:
            store(QKV + (b + 1) * OWN, g[:, 128:])
    for b in range(0, 4, 2):
        g = dot(mixed_t, whole("db", slice(128 * b, 128 * b + 256)))
        store(OUT + b * OWN, g[:, :128])
        store(OUT + (b + 1) * OWN, g[:, 128:])
    sums = r["gsum"][0] + r["gsum"][1]
    row = lax.broadcasted_iota(jnp.int32, (128, D), 0)
    store(GAIN, jnp.where(row == 0, sums[0:1], jnp.where(row == 1, sums[1:2], 0.0)).T)
    flat[0, USED:] = jnp.zeros((FLAT - USED, 128), BF16)
    flat[1, USED:] = jnp.zeros((FLAT - USED, 128), BF16)
    done(FLAT)


KEPT = {
    "wq": ((D, 1024), BF16),
    "wo": ((D, D), BF16),
    "wg": ((D, FF), BF16),
    "wu": ((D, FF), BF16),
    "wd": ((D, FF), BF16),
    "x": ((MICRO, ROWS, D), F32),
    "dy": ((MICRO, ROWS, D), F32),
    "lens": ((MICRO, 8, 128), F32),
    "lens_own": ((MICRO, 8, 128), F32),
    "lens_pair": ((MICRO, 8, 128), F32),
    "cot_pair": ((MICRO, D, ROWS), BF16),
    "y_send": ((MICRO, ROWS, D), BF16),
    "y_box": ((MICRO, ROWS, D), BF16),
    "y_turn": ((MICRO, D, ROWS), BF16),
    "dx_send": ((MICRO, ROWS, D), BF16),
    "dx_box": ((MICRO, ROWS, D), BF16),
    "dx_turn": ((MICRO, D, ROWS), BF16),
    "ent": ((MICRO, ROWS, D), BF16),
    "qs": ((MICRO, 3, 3 * ROWS, 128), BF16),
    "kd": ((MICRO, 3, ROWS, 128), BF16),
    "vd": ((MICRO, 3, ROWS, 128), BF16),
    "pr": ((MICRO, 3, 3 * ROWS, 128), F32),
    "mix": ((MICRO, ROWS, D), BF16),
    "mid": ((MICRO, ROWS, D), F32),
    "sec": ((MICRO, ROWS, D), BF16),
    "inn": ((MICRO, ROWS, FF), BF16),
    "fa": ((MICRO, ROWS, FF), F32),
    "fb": ((MICRO, ROWS, FF), F32),
    "cs": ((MICRO, ROWS, 128), F32),
    "sn": ((MICRO, ROWS, 128), F32),
    "df": ((MICRO, ROWS, D), BF16),
    "dg": ((MICRO, ROWS, FF), BF16),
    "du": ((MICRO, ROWS, FF), BF16),
    "db": ((MICRO, ROWS, D), BF16),
    "dqkv": ((MICRO, ROWS, 1024), BF16),
    "gsum": ((MICRO, 8, D), F32),
    "flat": ((2, FLAT, 128), BF16),
    "cross": ((8, P1, 128), BF16),
    "one": ((12, P1 // 2, 128), BF16),
    "two": ((12, P2 // 2, 128), BF16),
    "zed": ((2, P3, 128), BF16),
}
SEMS = {
    "w": 5,
    "swap": 2,
    "y": 2,
    "dx": 2,
    "y_swap": 2,
    "dx_swap": 2,
    "cross": 8,
    "one": 12,
    "two": 12,
    "zed": 4,
    "along": 12,
    "back": 24,
}


def vmem(n):
    return [pl.BlockSpec(memory_space=pltpu.VMEM)] * n


def hbm(n):
    return [pl.BlockSpec(memory_space=pl.ANY)] * n


def places():
    section, core, replica = (lax.axis_index(a) for a in ("section", "shard", "replica"))
    x, y, z = replica // 8, replica // 2 % 4, replica % 2

    def at(x_, y_, z_):
        return (section, core, x_ * 8 + y_ * 2 + z_)

    return {
        "section": section,
        "core": core,
        "x": x,
        "y": y,
        "z": z,
        "x_next": at((x + 1) % 4, y, z),
        "x_prev": at((x + 3) % 4, y, z),
        "y_next": at(x, (y + 1) % 4, z),
        "y_prev": at(x, (y + 3) % 4, z),
        "z_pair": at(x, y, 1 - z),
        "partner": (section, 1 - core, replica),
        "across": (1 - section, core, x * 8 + y * 2 + (1 - z)),
    }


def step_kernel(
    lens, tok, cot, gain_one, gain_two, wq_own, wk_own, wv_own, wo_own, wg_own, wu_own, wd_own,
    y_out, dx_out, o, *refs
):
    r = dict(zip(KEPT, refs))
    sends = dict(zip(SEMS, refs[len(KEPT) :]))
    recvs = dict(zip(SEMS, refs[len(KEPT) + len(SEMS) :]))
    local = refs[len(KEPT) + 2 * len(SEMS)]
    at = places()
    section, core = at["section"], at["core"]

    barrier = pltpu.get_barrier_semaphore()
    near = ("partner", "x_next", "x_prev", "y_next", "y_prev", "z_pair", "across")
    for name in near:
        pl.semaphore_signal(barrier, inc=1, device_id=at[name], device_id_type=MESH)
    pl.semaphore_wait(barrier, len(near))

    def remote(name, i, src, dst, device):
        return pltpu.make_async_remote_copy(
            src,
            dst,
            sends[name].at[i],
            recvs[name].at[i],
            device_id=at[device],
            device_id_type=MESH,
        )

    own_rows = pl.ds(pl.multiple_of(core * OWN, 16), OWN)
    own_cols = pl.ds(pl.multiple_of(core * (FF // 2), 128), FF // 2)
    weight_places = {
        "wo": (wo_own, r["wo"].at[own_rows]),
        "wg": (wg_own, r["wg"].at[own_rows]),
        "wu": (wu_own, r["wu"].at[own_rows]),
        "wd": (wd_own, r["wd"].at[:, own_cols]),
    }
    r["wq"][own_rows, :512] = wq_own[:, :512]
    for start, value in side_rows(wq_own, wk_own, wv_own, gain_one, gain_two).items():
        r["wq"][own_rows, start : start + 128] = value.astype(BF16)
    side_place = r["wq"].at[own_rows]
    weight_copies = {"side": [remote("w", 0, side_place, side_place, "partner")]}
    for i, (name, (src, dst)) in enumerate(weight_places.items()):
        weight_copies[name] = [
            remote("w", i + 1, src, dst, "partner"),
            pltpu.make_async_copy(src, dst, local.at[i]),
        ]
    for copies in weight_copies.values():
        for copy in copies:
            copy.start()

    r["lens_own"][...] = jnp.zeros((MICRO, 8, 128), F32)
    for m in range(MICRO):
        r["lens_own"][m, 0:1, 0:2] = lens[m : m + 1, :].astype(F32)
    lens_swap = remote("swap", 0, r["lens_own"], r["lens_pair"], "z_pair")
    cot_swap = remote("swap", 1, cot, r["cot_pair"], "z_pair")
    lens_swap.start()
    cot_swap.start()
    lens_swap.wait_recv()

    @pl.when(section == 0)
    def _():
        r["lens"][...] = r["lens_own"][...]

    @pl.when(section == 1)
    def _():
        r["lens"][...] = r["lens_pair"][...]

    def y_copy(m):
        return remote("y", m, r["y_send"].at[m], r["y_box"].at[m], "across")

    def dx_copy(m):
        return remote("dx", m, r["dx_send"].at[m], r["dx_box"].at[m], "across")

    def y_swap(m):
        return remote("y_swap", m, r["y_turn"].at[m], y_out.at[m], "z_pair")

    def dx_swap(m):
        return remote("dx_swap", m, r["dx_turn"].at[m], dx_out.at[m], "z_pair")

    def tick(t, carry):
        m = jnp.where(section == 0, t % 2, t // 2)
        ahead = jnp.where(section == 0, t // 2, t % 2) == 0

        @pl.when(ahead)
        def _():
            @pl.when(section == 0)
            def _():
                r["x"][m] = tok[m].astype(F32).T

            @pl.when(section == 1)
            def _():
                y_copy(m).wait_recv()
                r["x"][m] = r["y_box"][m].astype(F32)

            def arrived(name):
                @pl.when(t == 0)
                def _():
                    for i, copy in enumerate(weight_copies[name]):
                        if i == 0:
                            copy.wait_recv()
                        else:
                            copy.wait()

            y = forward(r, m, arrived)
            r["y_send"][m] = y.astype(BF16)

            @pl.when(section == 0)
            def _():
                y_copy(m).start()
                y_out[m] = r["y_send"][m].astype(F32).T.astype(BF16)

            @pl.when(section == 1)
            def _():
                r["y_turn"][m] = r["y_send"][m].astype(F32).T.astype(BF16)
                y_swap(m).start()

        @pl.when(jnp.logical_not(ahead))
        def _():
            @pl.when(section == 0)
            def _():
                dx_copy(m).wait_recv()
                r["dy"][m] = r["dx_box"][m].astype(F32)

            @pl.when(section == 1)
            def _():
                @pl.when(t == 1)
                def _():
                    cot_swap.wait_recv()

                ids = lax.broadcasted_iota(jnp.int32, (ROWS, D), 0)
                live = ids < lengths_of(r, m)[1]
                r["dy"][m] = jnp.where(live, r["cot_pair"][m].astype(F32).T, 0.0)

            r["dx_send"][m] = backward(r, m).astype(BF16)

            @pl.when(section == 0)
            def _():
                dx_out[m] = r["dx_send"][m].astype(F32).T.astype(BF16)

            @pl.when(section == 1)
            def _():
                dx_copy(m).start()
                r["dx_turn"][m] = r["dx_send"][m].astype(F32).T.astype(BF16)
                dx_swap(m).start()

        return carry

    lax.fori_loop(0, 2 * MICRO, tick, 0)

    @pl.when(section == 0)
    def _():
        cot_swap.wait_recv()

    total = Total(r, o, at, remote)
    weight_grads(r, r["flat"], total.ready)
    total.reduce()
    total.spread()
    total.finish()

    lens_swap.wait_send()
    cot_swap.wait_send()
    for copies in weight_copies.values():
        copies[0].wait_send()

    @pl.when(section == 0)
    def _():
        for m in range(MICRO):
            y_copy(m).wait_send()

    @pl.when(section == 1)
    def _():
        for m in range(MICRO):
            dx_copy(m).wait_send()
            y_swap(m).wait()
            dx_swap(m).wait()


def span(start, count):
    return pl.ds(pl.multiple_of(start, 16), count)


class Total:
    def __init__(self, r, o, at, remote):
        self.flat, self.box, self.one, self.two, self.zed = (
            r[k] for k in ("flat", "cross", "one", "two", "zed")
        )
        self.o, self.at, self.remote = o, at, remote
        self.core, self.z = at["core"], at["z"]
        self.pos = ((at["x"], at["y"]), (at["y"], at["x"]))
        xs, ys = ("x_next", "x_prev"), ("y_next", "y_prev")
        self.dev = ((xs, ys), (ys, xs))
        self.sent, self.cross = [], {}

    def send(self, name, i, src, dst, device):
        copy = self.remote(name, i, src, dst, device)
        copy.start()
        self.sent.append(copy)
        return copy

    def ready(self, rows):
        while len(self.cross) < 8 and P1 * (len(self.cross) + 1) <= rows:
            i = len(self.cross)
            src = self.flat.at[1 - self.core, P1 * i : P1 * (i + 1)]
            self.cross[i] = self.send("cross", i, src, self.box.at[i], "partner")

    def rows(self, h, k, start=0, count=P1):
        return span(HALF * h + P1 * ((self.pos[h][0] + k) % 4) + start, count)

    def add(self, h, k, start, count, *others):
        rows = self.rows(h, k, start, count)
        box = self.box[h * 4 + (self.pos[h][0] + k) % 4, start : start + count]
        value = self.flat[self.core, rows].astype(F32) + box.astype(F32)
        for other in others:
            value = value + other.astype(F32)
        self.flat[self.core, rows] = value.astype(BF16)
        return self.flat.at[self.core, rows]

    def piece(self, h, k):
        return P2 * ((self.pos[h][1] + k) % 4)

    def add_two(self, h, k, start, *others):
        rows = self.rows(h, 0, self.piece(h, k) + start, P2 // 2)
        value = self.flat[self.core, rows].astype(F32)
        for other in others:
            value = value + other.astype(F32)
        self.flat[self.core, rows] = value.astype(BF16)
        return self.flat.at[self.core, rows]

    def reduce(self):
        h1, h2 = P1 // 2, P2 // 2
        one, two = {}, {}

        def go1(h, i, ref, way):
            buf = self.one.at[h * 6 + i]
            one[h, i] = self.send("one", h * 6 + i, ref, buf, self.dev[h][0][way])

        def go2(h, i, ref, way):
            buf = self.two.at[h * 6 + i]
            two[h, i] = self.send("two", h * 6 + i, ref, buf, self.dev[h][1][way])

        def got1(h, i):
            one[h, i].wait_recv()
            return self.one[h * 6 + i]

        def got2(h, i):
            two[h, i].wait_recv()
            return self.two[h * 6 + i]

        for h in range(2):
            for q in range(4):
                self.cross[h * 4 + q].wait_recv()
            go1(h, 0, self.add(h, 2, 0, h1), 0)
            go1(h, 1, self.add(h, 2, h1, h1), 1)
            go1(h, 2, self.add(h, 1, h1, h1), 0)
            go1(h, 3, self.add(h, 3, 0, h1), 1)
        for h in range(2):
            go1(h, 4, self.add(h, 1, 0, h1, got1(h, 0)), 0)
            go1(h, 5, self.add(h, 3, h1, h1, got1(h, 1)), 1)
        for h in range(2):
            self.add(h, 0, 0, h1, got1(h, 3), got1(h, 4))
            self.add(h, 0, h1, h1, got1(h, 2), got1(h, 5))

            def part(k, start):
                return self.flat.at[self.core, self.rows(h, 0, self.piece(h, k) + start, h2)]

            go2(h, 0, part(2, 0), 0)
            go2(h, 1, part(2, h2), 1)
            go2(h, 2, part(1, h2), 0)
            go2(h, 3, part(3, 0), 1)
        for h in range(2):
            go2(h, 4, self.add_two(h, 1, 0, got2(h, 0)), 0)
            go2(h, 5, self.add_two(h, 3, h2, got2(h, 1)), 1)
        self.z_copies = {}
        for h in range(2):
            self.add_two(h, 0, 0, got2(h, 3), got2(h, 4))
            self.add_two(h, 0, h2, got2(h, 2), got2(h, 5))
            rows = self.rows(h, 0, self.piece(h, 0) + P3 * (1 - self.z), P3)
            self.z_copies[h] = self.send(
                "zed", h, self.flat.at[self.core, rows], self.zed.at[h], "z_pair"
            )

    def block(self, h, k1, k2, part=None):
        start = self.piece(h, k2)
        if part is None:
            return self.o.at[self.rows(h, k1, start, P2)]
        return self.o.at[self.rows(h, k1, start + P3 * ((self.z + part) % 2), P3)]

    def spread(self):
        along, back, ahead = {}, {}, {}

        def give(name, i, ref, device):
            return self.send(name, i, ref, ref, device)

        def give_first(h, k):
            for d in range(2):
                back[h, d, k] = give(
                    "back", h * 12 + d * 6 + k, self.block(h, 0, k), self.dev[h][0][d]
                )

        def give_second(h, k):
            for d in range(2):
                along[h, d, k] = give(
                    "along", h * 6 + d * 3 + k, self.block(h, 0, 0, k), self.dev[h][1][d]
                )

        for h in range(2):
            self.z_copies[h].wait_recv()
            rows = self.rows(h, 0, self.piece(h, 0) + P3 * self.z, P3)
            value = self.flat[self.core, rows].astype(F32) + self.zed[h].astype(F32)
            self.o[rows] = value.astype(BF16)
            self.z_copies[h] = give("zed", 2 + h, self.block(h, 0, 0, 0), "z_pair")
            give_second(h, 0)
        for h in range(2):
            self.z_copies[h].wait_recv()
            give_second(h, 1)
            give_first(h, 0)
        for h in range(2):
            along[h, 0, 0].wait_recv()
            along[h, 0, 2] = give("along", h * 6 + 2, self.block(h, 0, 3, 0), self.dev[h][1][0])
            along[h, 1, 0].wait_recv()
            along[h, 1, 1].wait_recv()
            along[h, 1, 2] = give("along", h * 6 + 5, self.block(h, 0, 1, 1), self.dev[h][1][1])
            give_first(h, 1)
            along[h, 0, 1].wait_recv()
            give_first(h, 3)
        for h in range(2):
            along[h, 0, 2].wait_recv()
            along[h, 1, 2].wait_recv()
            give_first(h, 2)
        for k in (0, 1, 3, 2):
            for h in range(2):
                back[h, 0, k].wait_recv()
                back[h, 1, k].wait_recv()
                way = 0 if k in (0, 3) else 1
                ahead[h, k] = give(
                    "back",
                    h * 12 + way * 6 + (4 if k < 2 else 5),
                    self.block(h, 1 if way else 3, k),
                    self.dev[h][0][way],
                )
        for copy in ahead.values():
            copy.wait_recv()

    def finish(self):
        for copy in self.sent:
            copy.wait_send()


def run_step(lens, tok, cot, gain_one, gain_two, wq, wk, wv, wo, wg, wu, wd):
    rows = jax.ShapeDtypeStruct((MICRO, D, ROWS), BF16)
    sems = [pltpu.SemaphoreType.DMA((n,)) for n in SEMS.values()]
    return pl.pallas_call(
        step_kernel,
        out_shape=[rows, rows, jax.ShapeDtypeStruct((FLAT, 128), BF16)],
        in_specs=vmem(8) + hbm(4),
        out_specs=vmem(3),
        scratch_shapes=[pltpu.VMEM(*v) for v in KEPT.values()]
        + sems
        + sems
        + [pltpu.SemaphoreType.DMA((4,))],
        compiler_params=pltpu.CompilerParams(
            collective_id=1, has_side_effects=True, vmem_limit_bytes=VMEM_LIMIT
        ),
    )(lens, tok, cot, gain_one, gain_two, wq, wk, wv, wo, wg, wu, wd)


def unpack_kernel(f, y, dx, y_out, dx_out, gain_one, wq, wk, wv, wo, gain_two, wg, wu, wd):
    def rows(start, count=OWN):
        return f[start : start + count].astype(F32)

    y_out[...] = y[...]
    dx_out[...] = dx[...]
    for b in range(12):
        cols = slice(128 * b, 128 * b + 128)
        wg[0, :, cols] = rows(GATE + b * OWN)
        wu[0, :, cols] = rows(UP + b * OWN)
    for b in range(6):
        wd[0, :, 128 * b : 128 * b + 128] = rows(DOWN + b * D, D)
    for b in range(4):
        wq[0, :, 128 * b : 128 * b + 128] = rows(QKV + b * OWN)
        wo[0, :, 128 * b : 128 * b + 128] = rows(OUT + b * OWN)
    swap = [pltpu.roll(rows(QKV + b * OWN), 64, 1) for b in range(4, 8)]
    wq[0, :, 512:576] = rows(QKV + 4 * OWN)[:, :64]
    lane = lax.broadcasted_iota(jnp.int32, (OWN, 128), 1)
    wk[0, :, :128] = jnp.where(lane < 64, swap[0], swap[1])
    wk[0, :, 128:] = swap[1][:, :64]
    wv[0, :, :128] = rows(QKV + 6 * OWN)
    wv[0, :, 128:] = rows(QKV + 7 * OWN)[:, :64]
    wo[0, :, 512:576] = swap[3][:, :64]
    gains = rows(GAIN).T
    gain_one[...] = gains[0:1]
    gain_two[...] = gains[1:2]


def run_unpack(flat, y, dx):
    kinds = [(1, OWN), (1, OWN, D), (1, OWN, 192), (1, OWN, 192), (1, OWN, D)]
    kinds += [(1, OWN), (1, OWN, FF), (1, OWN, FF), (1, D, FF // 2)]
    return pl.pallas_call(
        unpack_kernel,
        out_shape=[jax.ShapeDtypeStruct(a.shape, a.dtype) for a in (y, dx)]
        + [jax.ShapeDtypeStruct(k, F32) for k in kinds],
        in_specs=vmem(3),
        out_specs=vmem(11),
        compiler_params=pltpu.CompilerParams(vmem_limit_bytes=VMEM_LIMIT),
    )(flat, y, dx)


def shards(
    tokens,
    cotangent,
    seq_lengths,
    gain_attn,
    w_query,
    w_key,
    w_value,
    w_out,
    gain_ffn,
    w_gate,
    w_up,
    w_down,
):
    y, dx, flat = run_step(
        seq_lengths,
        jnp.swapaxes(tokens, 1, 2),
        jnp.swapaxes(cotangent, 1, 2),
        gain_attn,
        gain_ffn,
        w_query[0],
        w_key[0],
        w_value[0],
        w_out[0],
        w_gate[0],
        w_up[0],
        w_down[0].T,
    )
    y, dx, *grads = run_unpack(flat, y, dx)
    grads[8] = jnp.swapaxes(grads[8], 1, 2)
    return (jnp.swapaxes(y, 1, 2)[None], jnp.swapaxes(dx, 1, 2)[None], *grads)


def solution(mesh):
    row_spec = P(None, ("shard", "replica"), None)
    out_spec = P("section", None, ("shard", "replica"), None)
    vector = P("section", "shard")
    matrix = P("section", "shard", None)
    weight_specs = (vector, matrix, matrix, matrix, matrix, vector, matrix, matrix, matrix)
    return jax.shard_map(
        shards,
        mesh=mesh,
        in_specs=(row_spec, row_spec, P(None, ("shard", "replica")), *weight_specs),
        out_specs=(out_spec, out_spec, *weight_specs),
        check_vma=False,
    )
```

```python
import functools
import math
from types import SimpleNamespace

import jax
import jax.numpy as jnp
from jax import lax
from jax.experimental import pallas as pl
from jax.experimental.pallas import tpu as pltpu
from jax.sharding import PartitionSpec as P

MESH = pl.DeviceIdType.MESH
F32 = jnp.float32
BF16 = jnp.bfloat16

D = 576
HD = 64
FF = 1536
ROWS = 128
MICRO = 2
M = MICRO * ROWS
OWN = D // 2
EPS = 1e-05
BASE = 100000.0
VMEM_LIMIT = 62 * 1024 * 1024

GATE = 0
UP = GATE + 12 * OWN
DOWN = UP + 12 * OWN
QKV = DOWN + 6 * D
OUT = QKV + 8 * OWN
GAIN = OUT + 4 * OWN
USED = GAIN + OWN
FLAT = 14336
CHUNKS = (5120, 5120, 4096)
PARTS = 2 * len(CHUNKS)
SIZE = [n // 2 for n in CHUNKS for _ in range(2)]
BASE_ROW = [sum(SIZE[:i]) for i in range(PARTS)]


def dot(a, b):
    return lax.dot_general(a, b, (((1,), (0,)), ((), ())), preferred_element_type=F32)


def dot_nt(a, b):
    return lax.dot_general(a, b, (((1,), (1,)), ((), ())), preferred_element_type=F32)


def dot_tn(a, b):
    return lax.dot_general(a, b, (((0,), (0,)), ((), ())), preferred_element_type=F32)


def lanes():
    return lax.broadcasted_iota(jnp.int32, (ROWS, 128), 1)


def slots():
    return lax.broadcasted_iota(jnp.int32, (ROWS, 128), 0)


def segment_of(ids, first_end, last_end):
    return jnp.where(ids >= first_end, 1, 0) + jnp.where(ids >= last_end, 1, 0)


def turned(u, lane):
    return jnp.where(lane % 64 < 32, pltpu.roll(u, 96, 1), pltpu.roll(u, 32, 1))


def both_halves(u, half, lane):
    return jnp.where(lane // 64 == half, u, pltpu.roll(u, 64, 1))


def norm_scale(x):
    return lax.rsqrt(jnp.mean(x * x, axis=-1, keepdims=True) + EPS)


def norm_back(upper, normed, scale):
    return scale * (upper - normed * jnp.mean(upper * normed, axis=-1, keepdims=True))


def lengths_of(r, m):
    first = r.lens[m, 0:1, 0:1].astype(jnp.int32)
    return first, first + r.lens[m, 0:1, 1:2].astype(jnp.int32)


def tables(r, m):
    first_end, last_end = lengths_of(r, m)
    lane, slot = lanes(), slots()
    inverse = jnp.exp((lane % 32).astype(F32) * (-2.0 * math.log(BASE) / HD))
    position = slot - jnp.where(slot >= first_end, first_end, 0)
    position = position - jnp.where(slot >= last_end, last_end - first_end, 0)
    angle = position.astype(F32) * inverse
    sine = jnp.sin(angle)
    r.cs[m] = jnp.cos(angle)
    r.sn[m] = jnp.where(lane % 64 < 32, -sine, sine)


def side_rows(wq, wk, wv, gain_one, gain_two):
    lane = lax.broadcasted_iota(jnp.int32, (OWN, 128), 1)
    none = jnp.zeros((OWN, 64), F32)
    tail = jnp.concatenate([wq[:, 512:576].astype(F32), none], axis=1)
    key_a = pltpu.roll(wk[:, :128].astype(F32), 64, 1)
    key_b = pltpu.roll(jnp.concatenate([wk[:, 128:192].astype(F32), none], axis=1), 64, 1)
    last = jnp.concatenate([wv[:, 128:192].astype(F32), none], axis=1)
    row = lax.broadcasted_iota(jnp.int32, (128, OWN), 0)
    gains = jnp.where(
        row == 64, gain_one[...].astype(F32), jnp.where(row == 65, gain_two[...].astype(F32), 0.0)
    ).T
    return {
        512: jnp.where(lane < 64, tail, key_a),
        640: jnp.where(lane < 64, key_a, key_b),
        768: wv[:, :128].astype(F32),
        896: last + gains,
    }


def forward(r, m, arrived):
    x = r.x[m]
    n1 = x * norm_scale(x)
    wq, wo, wg, wu, wd = r.wq, r.wo, r.wg, r.wu, r.wd
    g1, g2 = r.gains[0:1, :], r.gains[1:2, :]
    entry = (n1 * g1).astype(BF16)
    r.ent[m] = entry
    qkv = dot(entry, wq[...])
    lane = lanes()
    cosine, sine = r.cs[m], r.sn[m]
    first_end, last_end = lengths_of(r, m)
    allowed = (
        segment_of(slots(), first_end, last_end) == segment_of(lane, first_end, last_end)
    ) & (lane <= slots())
    allowed = jnp.concatenate([allowed.astype(F32)] * 3, axis=0) > 0.5
    blocks = []
    for b in range(6):
        u = qkv[:, 128 * b : 128 * b + 128]
        blocks.append(u * cosine + turned(u, lane) * sine)
    groups = range(3)
    keys = [both_halves(blocks[(9 + g) // 2], (9 + g) % 2, lane).astype(BF16) for g in groups]
    values = [
        both_halves(qkv[:, 768 + 128 * (g // 2) : 896 + 128 * (g // 2)], g % 2, lane).astype(BF16)
        for g in groups
    ]
    queries = [
        jnp.concatenate(
            [
                jnp.where(lane // 64 == j % 2, blocks[j // 2], 0.0).astype(BF16)
                for j in range(3 * g, 3 * g + 3)
            ],
            axis=0,
        )
        for g in groups
    ]
    scores = [
        jnp.where(allowed, dot_nt(q, k) * HD**-0.5, -1e30) for q, k in zip(queries, keys)
    ]
    tops = [jnp.max(v, axis=-1, keepdims=True) for v in scores]
    weights = [jnp.exp(v - top) for v, top in zip(scores, tops)]
    sums = [jnp.sum(w, axis=-1, keepdims=True) for w in weights]
    probs = [w / total for w, total in zip(weights, sums)]
    outs = [dot(p.astype(BF16), v) for p, v in zip(probs, values)]
    heads = [out[ROWS * j : ROWS * (j + 1)] for out in outs for j in range(3)]
    for g in groups:
        r.kd[m, g] = keys[g]
        r.vd[m, g] = values[g]
        r.qs[m, g] = queries[g]
        r.pr[m, g] = probs[g]
    for b in range(4):
        r.mix[m, :, 128 * b : 128 * b + 128] = jnp.where(
            lane < 64, heads[2 * b], heads[2 * b + 1]
        ).astype(BF16)
    r.mix[m, :, 512:576] = heads[8][:, :64].astype(BF16)
    arrived("wo")
    middle = x + dot(r.mix[m], wo[...])
    r.mid[m] = middle
    second = (middle * norm_scale(middle) * g2).astype(BF16)
    r.sec[m] = second
    for j in range(0, FF, 256):
        cols = slice(j, j + 256)
        if j % (FF // 2) == 0:
            arrived("wg" + str(j))
            arrived("wu" + str(j))
        gate = dot(second, wg[:, cols])
        up = dot(second, wu[:, cols])
        sig = 1.0 / (1.0 + jnp.exp(-gate))
        swish = gate * sig
        r.inn[m, :, cols] = (swish * up).astype(BF16)
        r.fa[m, :, cols] = up * sig * (1.0 + gate * (1.0 - sig))
        r.fb[m, :, cols] = swish
    arrived("wd")
    return middle + dot_nt(r.inn[m], wd[...])


def backward(r, m, halfway):
    wq, wo, wg, wu, wd = r.wq, r.wo, r.wg, r.wu, r.wd
    g1, g2 = r.gains[0:1, :], r.gains[1:2, :]
    dy = r.dy[m]
    middle = r.mid[m]
    scale_two = norm_scale(middle)
    n2 = middle * scale_two
    df = dy.astype(BF16)
    r.df[m] = df
    for j in range(0, FF, 256):
        cols = slice(j, j + 256)
        d_inner = dot(df, wd[:, cols])
        r.dg[m, :, cols] = (d_inner * r.fa[m, :, cols]).astype(BF16)
        r.du[m, :, cols] = (d_inner * r.fb[m, :, cols]).astype(BF16)
    halfway()
    d_second = dot_nt(r.dg[m], wg[...]) + dot_nt(r.du[m], wu[...])
    r.gsum[m, 1:2, :] = jnp.sum(d_second * n2, axis=0, keepdims=True)
    d_middle = dy + norm_back(d_second * g2, n2, scale_two)
    branch = d_middle.astype(BF16)
    r.db[m] = branch
    d_mixed = dot_nt(branch, wo[...])
    lane = lanes()
    cosine, sine = r.cs[m], r.sn[m]
    groups = range(3)
    uppers = []
    for g in groups:
        parts = []
        for j in range(3 * g, 3 * g + 3):
            if j < 8:
                block = d_mixed[:, 128 * (j // 2) : 128 * (j // 2) + 128]
                block = jnp.where(lane // 64 == j % 2, block, 0.0)
            else:
                block = jnp.concatenate([d_mixed[:, 512:576], jnp.zeros((ROWS, 64), F32)], axis=1)
            parts.append(block.astype(BF16))
        uppers.append(jnp.concatenate(parts, axis=0))
    probs = [r.pr[m, g] for g in groups]
    d_probs = [dot_nt(uppers[g], r.vd[m, g]) for g in groups]
    dv = [dot_tn(probs[g].astype(BF16), uppers[g]) for g in groups]
    totals = [jnp.sum(d_probs[g] * probs[g], axis=-1, keepdims=True) for g in groups]
    d_scores = [
        (probs[g] * (d_probs[g] - totals[g]) * HD**-0.5).astype(BF16) for g in groups
    ]
    queries = [dot(d_scores[g], r.kd[m, g]) for g in groups]
    dk = [dot_tn(d_scores[g], r.qs[m, g]) for g in groups]
    dq = [q[ROWS * j : ROWS * (j + 1)] for q in queries for j in range(3)]
    dk = [key + pltpu.roll(key, 64, 1) for key in dk]
    dv = [value + pltpu.roll(value, 64, 1) for value in dv]
    heads = dq + dk
    for b in range(6):
        u = jnp.where(lane < 64, heads[2 * b], heads[2 * b + 1])
        r.dqkv[m, :, 128 * b : 128 * b + 128] = (u * cosine - turned(u, lane) * sine).astype(
            BF16
        )
    r.dqkv[m, :, 768:896] = jnp.where(lane < 64, dv[0], dv[1]).astype(BF16)
    r.dqkv[m, :, 896:1024] = jnp.where(lane < 64, dv[2], 0.0).astype(BF16)
    d_entry = dot_nt(r.dqkv[m], wq[...])
    x = r.x[m]
    scale_one = norm_scale(x)
    n1 = x * scale_one
    r.gsum[m, 0:1, :] = jnp.sum(d_entry * n1, axis=0, keepdims=True)
    return d_middle + norm_back(d_entry * g1, n1, scale_one)


def whole(ref, cols=slice(None)):
    value = ref[:, :, cols]
    return value.reshape(M, value.shape[-1])


def store(flat, start, block):
    flat[0, start : start + OWN] = block[:OWN].astype(BF16)
    flat[1, start : start + OWN] = block[OWN:].astype(BF16)


def gate_grads(r, flat, done):
    second_t = whole(r.sec).T
    for ref, start in ((r.dg, GATE), (r.du, UP)):
        for b in range(0, 12, 2):
            g = dot(second_t, whole(ref, slice(128 * b, 128 * b + 256)))
            store(flat, start + b * OWN, g[:, :128])
            store(flat, start + (b + 1) * OWN, g[:, 128:])
            done(start + (b + 2) * OWN)


def down_grads(r, flat, done):
    df_t = whole(r.df).T
    for b in range(6):
        for owner in range(2):
            first = 768 * owner + 128 * b
            g = dot(df_t, whole(r.inn, slice(first, first + 128)))
            flat[owner, DOWN + b * D : DOWN + (b + 1) * D] = g.astype(BF16)
        done(DOWN + (b + 1) * D)


def rest_grads(r, flat, done):
    entry_t = whole(r.ent).T
    mixed_t = whole(r.mix).T
    for b in range(0, 8, 2):
        g = dot(entry_t, whole(r.dqkv, slice(128 * b, 128 * b + 256)))
        store(flat, QKV + b * OWN, g[:, :128])
        if b == 6:
            rest = whole(r.db, slice(512, 576)).astype(F32)
            rest = jnp.concatenate([rest, jnp.zeros((M, 64), F32)], axis=1)
            rest = pltpu.roll(rest, 64, 1).astype(BF16)
            store(flat, QKV + 7 * OWN, g[:, 128:] + dot(mixed_t, rest))
        else:
            store(flat, QKV + (b + 1) * OWN, g[:, 128:])
        done(QKV + (b + 2) * OWN)
    for b in range(0, 4, 2):
        g = dot(mixed_t, whole(r.db, slice(128 * b, 128 * b + 256)))
        store(flat, OUT + b * OWN, g[:, :128])
        store(flat, OUT + (b + 1) * OWN, g[:, 128:])
        done(OUT + (b + 2) * OWN)
    sums = r.gsum[0] + r.gsum[1]
    row = lax.broadcasted_iota(jnp.int32, (128, D), 0)
    store(flat, GAIN, jnp.where(row == 0, sums[0:1], jnp.where(row == 1, sums[1:2], 0.0)).T)
    flat[0, USED:] = jnp.zeros((FLAT - USED, 128), BF16)
    flat[1, USED:] = jnp.zeros((FLAT - USED, 128), BF16)
    done(FLAT)


KEPT = dict(
    wq=((D, 1024), BF16),
    wo=((D, D), BF16),
    wg=((D, FF), BF16),
    wu=((D, FF), BF16),
    wd=((D, FF), BF16),
    gains=((8, D), F32),
    x=((MICRO, ROWS, D), F32),
    dy=((MICRO, ROWS, D), F32),
    lens=((MICRO, 8, 128), F32),
    lens_own=((MICRO, 8, 128), F32),
    lens_pair=((MICRO, 8, 128), F32),
    cot_pair=((MICRO, D, ROWS), BF16),
    y_send=((MICRO, ROWS, D), BF16),
    y_box=((MICRO, ROWS, D), BF16),
    y_turn=((MICRO, D, ROWS), BF16),
    dx_send=((MICRO, ROWS, D), BF16),
    dx_box=((MICRO, ROWS, D), BF16),
    dx_turn=((MICRO, D, ROWS), BF16),
    ent=((MICRO, ROWS, D), BF16),
    qs=((MICRO, 3, 3 * ROWS, 128), BF16),
    kd=((MICRO, 3, ROWS, 128), BF16),
    vd=((MICRO, 3, ROWS, 128), BF16),
    pr=((MICRO, 3, 3 * ROWS, 128), F32),
    mix=((MICRO, ROWS, D), BF16),
    mid=((MICRO, ROWS, D), F32),
    sec=((MICRO, ROWS, D), BF16),
    inn=((MICRO, ROWS, FF), BF16),
    fa=((MICRO, ROWS, FF), F32),
    fb=((MICRO, ROWS, FF), F32),
    cs=((MICRO, ROWS, 128), F32),
    sn=((MICRO, ROWS, 128), F32),
    df=((MICRO, ROWS, D), BF16),
    dg=((MICRO, ROWS, FF), BF16),
    du=((MICRO, ROWS, FF), BF16),
    db=((MICRO, ROWS, D), BF16),
    dqkv=((MICRO, ROWS, 1024), BF16),
    gsum=((MICRO, 8, D), F32),
    flat=((2, FLAT, 128), BF16),
    cross=((FLAT, 128), BF16),
    one=((6 * PARTS, max(SIZE) // 8, 128), BF16),
    two=((7 * PARTS, max(SIZE) // 32, 128), BF16),
    o=((FLAT, 128), BF16),
)
SEMS = dict(
    w=7,
    swap=2,
    y=2,
    dx=2,
    y_swap=2,
    dx_swap=2,
    cross=4 * PARTS,
    one=6 * PARTS,
    two=7 * PARTS,
    along=7 * PARTS,
    back=12 * PARTS,
)


def vmem(n):
    return [pl.BlockSpec(memory_space=pltpu.VMEM)] * n


def hbm(n):
    return [pl.BlockSpec(memory_space=pl.ANY)] * n


PLANE = [(0, 1), (1, 0), (3, 0), (1, 1), (3, 1), (2, 0), (2, 1)]


def places():
    section, core, replica = (lax.axis_index(a) for a in ("section", "shard", "replica"))
    x, y, z = replica // 8, replica // 2 % 4, replica % 2

    def at(x_, y_, z_):
        return (section, core, x_ * 8 + y_ * 2 + z_)

    return SimpleNamespace(
        section=section,
        core=core,
        x=x,
        y=y,
        z=z,
        x_next=at((x + 1) % 4, y, z),
        x_prev=at((x + 3) % 4, y, z),
        y_next=at(x, (y + 1) % 4, z),
        y_prev=at(x, (y + 3) % 4, z),
        z_pair=at(x, y, 1 - z),
        x_plane=[at((x + k) % 4, y, (z + w) % 2) for k, w in PLANE],
        y_plane=[at(x, (y + k) % 4, (z + w) % 2) for k, w in PLANE],
        partner=(section, 1 - core, replica),
        across=(1 - section, core, x * 8 + y * 2 + (1 - z)),
    )


def step_kernel(
    lens, tok, cot, gain_one, gain_two, wq_own, wk_own, wv_own, wo_own, wg_own, wu_own, wd_own,
    y_out, dx_out, o, *refs
):
    r = SimpleNamespace(**dict(zip(KEPT, refs)))
    sends = dict(zip(SEMS, refs[len(KEPT) :]))
    recvs = dict(zip(SEMS, refs[len(KEPT) + len(SEMS) :]))
    local = refs[len(KEPT) + 2 * len(SEMS)]
    at = places()
    section, core = at.section, at.core

    barrier = pltpu.get_barrier_semaphore()
    near = [at.partner, at.across, *at.x_plane, *at.y_plane[1:]]
    for device in near:
        pl.semaphore_signal(barrier, inc=1, device_id=device, device_id_type=MESH)
    def remote(name, i, src, dst, device):
        return pltpu.make_async_remote_copy(
            src,
            dst,
            sends[name].at[i],
            recvs[name].at[i],
            device_id=device,
            device_id_type=MESH,
        )

    own_rows = pl.ds(pl.multiple_of(core * OWN, 16), OWN)
    own_cols = pl.ds(pl.multiple_of(core * (FF // 2), 128), FF // 2)
    weight_places = {"wo": (wo_own, r.wo.at[own_rows])}
    for j in range(0, FF, FF // 2):
        cols = slice(j, j + FF // 2)
        weight_places["wg" + str(j)] = (wg_own.at[:, cols], r.wg.at[own_rows, cols])
        weight_places["wu" + str(j)] = (wu_own.at[:, cols], r.wu.at[own_rows, cols])
    weight_places["wd"] = (wd_own, r.wd.at[:, own_cols])
    side_place = r.wq.at[own_rows]
    weight_copies = {"side": [remote("w", 0, side_place, side_place, at.partner)]}
    for i, (name, (src, dst)) in enumerate(weight_places.items()):
        weight_copies[name] = [
            remote("w", i + 1, src, dst, at.partner),
            pltpu.make_async_copy(src, dst, local.at[i]),
        ]
        weight_copies[name][1].start()
    r.wq[own_rows, :512] = wq_own[:, :512]
    for start, value in side_rows(wq_own, wk_own, wv_own, gain_one, gain_two).items():
        r.wq[own_rows, start : start + 128] = value.astype(BF16)

    r.lens_own[...] = jnp.zeros((MICRO, 8, 128), F32)
    for m in range(MICRO):
        r.lens_own[m, 0:1, 0:2] = lens[m : m + 1, :].astype(F32)
    lens_swap = remote("swap", 0, r.lens_own, r.lens_pair, at.z_pair)
    cot_swap = remote("swap", 1, cot, r.cot_pair, at.z_pair)

    pl.semaphore_wait(barrier, len(near))
    for name in ("side", "wo"):
        weight_copies[name][0].start()
    lens_swap.start()
    cot_swap.start()

    @pl.when(section == 0)
    def _():
        r.lens[...] = r.lens_own[...]
        for m in range(MICRO):
            r.x[m] = tok[m].astype(F32).T

    @pl.when(section == 1)
    def _():
        lens_swap.wait_recv()
        r.lens[...] = r.lens_pair[...]

    for m in range(MICRO):
        tables(r, m)
    weight_copies["side"][0].wait_recv()
    for name in weight_places:
        if name != "wo":
            weight_copies[name][0].start()
    r.gains[...] = r.wq[:, 896:1024].astype(F32).T[64:72]

    def y_copy(m):
        return remote("y", m, r.y_send.at[m], r.y_box.at[m], at.across)

    def dx_copy(m):
        return remote("dx", m, r.dx_send.at[m], r.dx_box.at[m], at.across)

    def y_swap(m):
        return remote("y_swap", m, r.y_turn.at[m], y_out.at[m], at.z_pair)

    def dx_swap(m):
        return remote("dx_swap", m, r.dx_turn.at[m], dx_out.at[m], at.z_pair)

    total = Total(r, at, remote)

    def tick(t, carry):
        m = jnp.where(section == 0, t % 2, t // 2)
        ahead = jnp.where(section == 0, t // 2, t % 2) == 0

        @pl.when(ahead)
        def _():
            @pl.when(section == 1)
            def _():
                y_copy(m).wait_recv()
                r.x[m] = r.y_box[m].astype(F32)

            def arrived(name):
                @pl.when(t == 0)
                def _():
                    for i, copy in enumerate(weight_copies[name]):
                        if i == 0:
                            copy.wait_recv()
                        else:
                            copy.wait()

            y = forward(r, m, arrived)
            r.y_send[m] = y.astype(BF16)

            @pl.when(section == 0)
            def _():
                y_copy(m).start()
                y_out[m] = r.y_send[m].astype(F32).T.astype(BF16)

            @pl.when(section == 1)
            def _():
                r.y_turn[m] = r.y_send[m].astype(F32).T.astype(BF16)
                y_swap(m).start()

        @pl.when(jnp.logical_not(ahead))
        def _():
            @pl.when(section == 0)
            def _():
                dx_copy(m).wait_recv()
                r.dy[m] = r.dx_box[m].astype(F32)

            @pl.when(section == 1)
            def _():
                @pl.when(t == 1)
                def _():
                    cot_swap.wait_recv()

                ids = lax.broadcasted_iota(jnp.int32, (ROWS, D), 0)
                live = ids < lengths_of(r, m)[1]
                r.dy[m] = jnp.where(live, r.cot_pair[m].astype(F32).T, 0.0)

            def halfway():
                @pl.when(jnp.logical_and(section == 0, t == 2 * MICRO - 1))
                def _():
                    gate_grads(r, r.flat, total.starter())

            r.dx_send[m] = backward(r, m, halfway).astype(BF16)

            @pl.when(section == 0)
            def _():
                dx_out[m] = r.dx_send[m].astype(F32).T.astype(BF16)

            @pl.when(section == 1)
            def _():
                dx_copy(m).start()
                r.dx_turn[m] = r.dx_send[m].astype(F32).T.astype(BF16)
                dx_swap(m).start()

        return carry

    lax.fori_loop(0, 2 * MICRO, tick, 0)

    @pl.when(section == 0)
    def _():
        lens_swap.wait_recv()
        cot_swap.wait_recv()

    @pl.when(section == 1)
    def _():
        gate_grads(r, r.flat, total.starter())

    started = total.starter(DOWN)
    total.step_1(0)
    down_grads(r, r.flat, started)
    rest_grads(r, r.flat, started)
    total.run(o, local)
    total.finish()

    lens_swap.wait_send()
    cot_swap.wait_send()
    for copies in weight_copies.values():
        copies[0].wait_send()

    @pl.when(section == 0)
    def _():
        for m in range(MICRO):
            y_copy(m).wait_send()

    @pl.when(section == 1)
    def _():
        for m in range(MICRO):
            dx_copy(m).wait_send()
            y_swap(m).wait()
            dx_swap(m).wait()


def span(start, count):
    return pl.ds(pl.multiple_of(start, 16), count)


class Total:
    def __init__(self, r, at, remote):
        self.flat, self.box, self.one, self.two, self.o = r.flat, r.cross, r.one, r.two, r.o
        self.at, self.remote = at, remote
        self.core = at.core
        self.pos = ((at.x, at.y), (at.y, at.x))
        xs, ys = (at.x_next, at.x_prev), (at.y_next, at.y_prev)
        self.first = (xs, ys)
        self.plane = (at.y_plane, at.x_plane)
        self.sent = []
        self.copies = {}

    def send(self, name, i, src, dst, device):
        copy = self.remote(name, i, src, dst, device)
        copy.start()
        self.sent.append(copy)
        self.copies[name, i] = copy

    def got(self, name, i):
        self.copies[name, i].wait_recv()

    def cross(self, n):
        i, q = n // 4, n % 4
        count = SIZE[i] // 4
        rows = slice(BASE_ROW[i] + q * count, BASE_ROW[i] + (q + 1) * count)
        src = self.flat.at[1 - self.core, rows]
        return self.remote("cross", n, src, self.box.at[rows], self.at.partner)

    def starter(self, first=0):
        ends = [BASE_ROW[n // 4] + (n % 4 + 1) * SIZE[n // 4] // 4 for n in range(4 * PARTS)]
        begun = [sum(end <= first for end in ends)]

        def ready(rows):
            while begun[0] < len(ends) and ends[begun[0]] <= rows:
                self.cross(begun[0]).start()
                begun[0] += 1

        return ready

    def rows(self, i, k, start=0, count=None):
        place = SIZE[i] // 4 * ((self.pos[i % 2][0] + k) % 4)
        return span(BASE_ROW[i] + place + start, count)

    def piece(self, i, k):
        return SIZE[i] // 16 * ((self.pos[i % 2][1] + k) % 4)

    def add(self, i, k, upper, *others):
        count = SIZE[i] // 8
        rows = self.rows(i, k, upper * count, count)
        value = self.flat[self.core, rows].astype(F32) + self.box[rows].astype(F32)
        for other in others:
            value = value + other.astype(F32)
        self.flat[self.core, rows] = value.astype(BF16)
        return self.flat.at[self.core, rows]

    def go(self, i, slot, ref, way):
        device = self.first[i % 2][way]
        box = self.one.at[i * 6 + slot, : SIZE[i] // 8]
        self.send("one", i * 6 + slot, ref, box, device)

    def box_of(self, i, slot):
        self.got("one", i * 6 + slot)
        return self.one[i * 6 + slot, : SIZE[i] // 8]

    def step_1(self, c):
        for i in (2 * c, 2 * c + 1):
            for q in range(4):
                self.cross(i * 4 + q).wait_recv()
            self.go(i, 0, self.add(i, 2, 0), 0)
            self.go(i, 1, self.add(i, 2, 1), 1)
        for i in (2 * c, 2 * c + 1):
            self.go(i, 2, self.add(i, 1, 1), 0)
            self.go(i, 3, self.add(i, 3, 0), 1)

    def step_2(self, c):
        for i in (2 * c, 2 * c + 1):
            self.go(i, 4, self.add(i, 1, 0, self.box_of(i, 0)), 0)
            self.go(i, 5, self.add(i, 3, 1, self.box_of(i, 1)), 1)

    def block(self, i, k, w):
        count = SIZE[i] // 32
        return self.rows(i, 0, self.piece(i, k) + count * ((self.at.z + w) % 2), count)

    def two_box(self, i, j):
        return self.two.at[i * 7 + j, : SIZE[i] // 32]

    def step_3(self, c):
        for i in (2 * c, 2 * c + 1):
            self.add(i, 0, 0, self.box_of(i, 3), self.box_of(i, 4))
            self.add(i, 0, 1, self.box_of(i, 2), self.box_of(i, 5))
            for j, (k, w) in enumerate(PLANE):
                src = self.flat.at[self.core, self.block(i, k, w)]
                self.send("two", i * 7 + j, src, self.two_box(i, j), self.plane[i % 2][j])

    def step_4(self, c):
        for i in (2 * c, 2 * c + 1):
            rows = self.block(i, 0, 0)
            value = self.flat[self.core, rows].astype(F32)
            for j in range(7):
                self.got("two", i * 7 + j)
                value = value + self.two[i * 7 + j, : SIZE[i] // 32].astype(F32)
            self.o[rows] = value.astype(BF16)
            ref = self.o.at[rows]
            for j in range(7):
                self.send("along", i * 7 + j, ref, ref, self.plane[i % 2][j])

    def unit(self, i, k1, k2):
        return self.o.at[self.rows(i, k1, self.piece(i, k2), SIZE[i] // 16)]

    def step_5(self, c):
        for k in (0, 1, 3, 2):
            for i in (2 * c, 2 * c + 1):
                for j, (there, _) in enumerate(PLANE):
                    if there == k:
                        self.got("along", i * 7 + j)
                back = (4 - k) % 4
                ref = self.unit(i, 0, back)
                for d in range(2):
                    self.send("back", i * 12 + d * 6 + back, ref, ref, self.first[i % 2][d])

    def step_6(self, c):
        for k in (0, 3, 1, 2):
            for i in (2 * c, 2 * c + 1):
                self.got("back", i * 12 + k)
                self.got("back", i * 12 + 6 + k)
                way = 0 if k in (0, 3) else 1
                ref = self.unit(i, 1 if way else 3, k)
                slot = i * 12 + way * 6 + (4 if k < 2 else 5)
                self.send("back", slot, ref, ref, self.first[i % 2][way])

    def step_7(self, c):
        for i in (2 * c, 2 * c + 1):
            for slot in (4, 5, 10, 11):
                self.got("back", i * 12 + slot)
        rows = slice(BASE_ROW[2 * c], BASE_ROW[2 * c] + CHUNKS[c])
        copy = pltpu.make_async_copy(self.o.at[rows], self.out.at[rows], self.sem.at[c])
        copy.start()
        self.written.append(copy)

    def run(self, out, sem):
        self.out, self.sem, self.written = out, sem, []
        for n in range(2, 7 + len(CHUNKS)):
            for c in range(len(CHUNKS)):
                if 1 <= n - c <= 7:
                    getattr(self, f"step_{n - c}")(c)
        for copy in self.written:
            copy.wait()

    def finish(self):
        for n in range(4 * PARTS):
            self.cross(n).wait_send()
        for copy in self.sent:
            copy.wait_send()


def run_step(lens, tok, cot, gain_one, gain_two, wq, wk, wv, wo, wg, wu, wd):
    rows = jax.ShapeDtypeStruct((MICRO, D, ROWS), BF16)
    sems = [pltpu.SemaphoreType.DMA((n,)) for n in SEMS.values()]
    return pl.pallas_call(
        step_kernel,
        out_shape=[rows, rows, jax.ShapeDtypeStruct((FLAT, 128), BF16)],
        in_specs=vmem(8) + hbm(4),
        out_specs=vmem(2) + hbm(1),
        scratch_shapes=[pltpu.VMEM(*v) for v in KEPT.values()]
        + sems
        + sems
        + [pltpu.SemaphoreType.DMA((6,))],
        compiler_params=pltpu.CompilerParams(
            collective_id=1, has_side_effects=True, vmem_limit_bytes=VMEM_LIMIT
        ),
    )(lens, tok, cot, gain_one, gain_two, wq, wk, wv, wo, wg, wu, wd)


def unpack_kernel(
    f, y, dx, y_out, dx_out, gain_one, wq, wk, wv, wo, gain_two, wg, wu, wd, *refs
):
    flat, s_y, s_dx, s_wq, s_wk, s_wv, s_wo, s_wg, s_wu, s_wd, arrive, leave = refs
    step = 6 * OWN
    bounds = (*range(0, QKV, step), QKV, USED)
    loads = []

    def load(src, dst):
        loads.append(pltpu.make_async_copy(src, dst, arrive.at[len(loads)]))
        loads[-1].start()

    for i in range(len(bounds) - 1):
        part = slice(bounds[i], bounds[i + 1])
        load(f.at[part], flat.at[part])
    load(y, s_y)
    load(dx, s_dx)
    stores = []

    def put(src, dst):
        stores.append(pltpu.make_async_copy(src, dst, leave.at[len(stores)]))
        stores[-1].start()

    def rows(start, count=OWN):
        return flat[start : start + count].astype(F32)

    n = 0
    for start, stage, dst in ((GATE, s_wg, wg), (UP, s_wu, wu)):
        for j in range(0, 12, 6):
            loads[n].wait()
            n += 1
            for b in range(j, j + 6):
                stage[:, 128 * b : 128 * b + 128] = rows(start + b * OWN)
            cols = slice(128 * j, 128 * j + 768)
            put(stage.at[:, cols], dst.at[0, :, cols])
    for j in range(0, 6, 3):
        loads[n].wait()
        n += 1
        for b in range(j, j + 3):
            s_wd[:, 128 * b : 128 * b + 128] = rows(DOWN + b * D, D)
        cols = slice(128 * j, 128 * j + 384)
        put(s_wd.at[:, cols], wd.at[0, :, cols])
    loads[n].wait()
    n += 1
    swap = [pltpu.roll(rows(QKV + b * OWN), 64, 1) for b in range(4, 8)]
    lane = lax.broadcasted_iota(jnp.int32, (OWN, 128), 1)
    for b in range(4):
        s_wq[:, 128 * b : 128 * b + 128] = rows(QKV + b * OWN)
        s_wo[:, 128 * b : 128 * b + 128] = rows(OUT + b * OWN)
    s_wq[:, 512:576] = rows(QKV + 4 * OWN)[:, :64]
    put(s_wq, wq.at[0])
    s_wo[:, 512:576] = swap[3][:, :64]
    put(s_wo, wo.at[0])
    s_wk[:, :128] = jnp.where(lane < 64, swap[0], swap[1])
    s_wk[:, 128:] = swap[1][:, :64]
    put(s_wk, wk.at[0])
    s_wv[:, :128] = rows(QKV + 6 * OWN)
    s_wv[:, 128:] = rows(QKV + 7 * OWN)[:, :64]
    put(s_wv, wv.at[0])
    for src, dst in ((s_y, y_out), (s_dx, dx_out)):
        loads[n].wait()
        n += 1
        put(src, dst)
    gains = rows(GAIN).T
    gain_one[...] = gains[0:1]
    gain_two[...] = gains[1:2]
    for copy in stores:
        copy.wait()


def run_unpack(flat, y, dx):
    kinds = [(1, OWN), (1, OWN, D), (1, OWN, 192), (1, OWN, 192), (1, OWN, D)]
    kinds += [(1, OWN), (1, OWN, FF), (1, OWN, FF), (1, D, FF // 2)]
    stages = [pltpu.VMEM(k[1:], F32) for k in kinds if len(k) == 3]
    return pl.pallas_call(
        unpack_kernel,
        out_shape=[jax.ShapeDtypeStruct(a.shape, a.dtype) for a in (y, dx)]
        + [jax.ShapeDtypeStruct(k, F32) for k in kinds],
        in_specs=hbm(3),
        out_specs=hbm(2) + [(vmem if len(k) == 2 else hbm)(1)[0] for k in kinds],
        scratch_shapes=[pltpu.VMEM((FLAT, 128), BF16)]
        + [pltpu.VMEM(y.shape, y.dtype)] * 2
        + stages
        + [pltpu.SemaphoreType.DMA((9,)), pltpu.SemaphoreType.DMA((12,))],
        compiler_params=pltpu.CompilerParams(vmem_limit_bytes=VMEM_LIMIT),
    )(flat, y, dx)


def shards(
    tokens,
    cotangent,
    seq_lengths,
    gain_attn,
    w_query,
    w_key,
    w_value,
    w_out,
    gain_ffn,
    w_gate,
    w_up,
    w_down,
):
    y, dx, flat = run_step(
        seq_lengths,
        jnp.swapaxes(tokens, 1, 2),
        jnp.swapaxes(cotangent, 1, 2),
        gain_attn,
        gain_ffn,
        w_query[0],
        w_key[0],
        w_value[0],
        w_out[0],
        w_gate[0],
        w_up[0],
        w_down[0].T,
    )
    y, dx, *grads = run_unpack(flat, y, dx)
    grads[8] = jnp.swapaxes(grads[8], 1, 2)
    return (jnp.swapaxes(y, 1, 2)[None], jnp.swapaxes(dx, 1, 2)[None], *grads)


def solution(mesh):
    row_spec = P(None, ("shard", "replica"), None)
    out_spec = P("section", None, ("shard", "replica"), None)
    vector = P("section", "shard")
    matrix = P("section", "shard", None)
    weight_specs = (vector, matrix, matrix, matrix, matrix, vector, matrix, matrix, matrix)
    return jax.shard_map(
        shards,
        mesh=mesh,
        in_specs=(row_spec, row_spec, P(None, ("shard", "replica")), *weight_specs),
        out_specs=(out_spec, out_spec, *weight_specs),
        check_vma=False,
    )
```

```python
import functools
import math
from types import SimpleNamespace

import jax
import jax.numpy as jnp
from jax import lax
from jax.experimental import pallas as pl
from jax.experimental.pallas import tpu as pltpu
from jax.sharding import PartitionSpec as P

MESH = pl.DeviceIdType.MESH
F32 = jnp.float32
BF16 = jnp.bfloat16

D = 576
HD = 64
FF = 1536
ROWS = 128
MICRO = 2
M = MICRO * ROWS
OWN = D // 2
EPS = 1e-05
BASE = 100000.0
VMEM_LIMIT = 62 * 1024 * 1024

GATE = 0
UP = GATE + 12 * OWN
DOWN = UP + 12 * OWN
QKV = DOWN + 6 * D
OUT = QKV + 8 * OWN
GAIN = OUT + 4 * OWN
USED = GAIN + OWN
FLAT = 14336
CHUNKS = (5120, 5120, 4096)
PARTS = 2 * len(CHUNKS)
SIZE = [n // 2 for n in CHUNKS for _ in range(2)]
BASE_ROW = [sum(SIZE[:i]) for i in range(PARTS)]


def dot(a, b):
    return lax.dot_general(a, b, (((1,), (0,)), ((), ())), preferred_element_type=F32)


def dot_nt(a, b):
    return lax.dot_general(a, b, (((1,), (1,)), ((), ())), preferred_element_type=F32)


def dot_tn(a, b):
    return lax.dot_general(a, b, (((0,), (0,)), ((), ())), preferred_element_type=F32)


def lanes():
    return lax.broadcasted_iota(jnp.int32, (ROWS, 128), 1)


def slots():
    return lax.broadcasted_iota(jnp.int32, (ROWS, 128), 0)


def segment_of(ids, first_end, last_end):
    return jnp.where(ids >= first_end, 1, 0) + jnp.where(ids >= last_end, 1, 0)


def turned(u, lane):
    return jnp.where(lane % 64 < 32, pltpu.roll(u, 96, 1), pltpu.roll(u, 32, 1))


def both_halves(u, half, lane):
    return jnp.where(lane // 64 == half, u, pltpu.roll(u, 64, 1))


def norm_scale(x):
    return lax.rsqrt(jnp.mean(x * x, axis=-1, keepdims=True) + EPS)


def norm_back(upper, normed, scale):
    return scale * (upper - normed * jnp.mean(upper * normed, axis=-1, keepdims=True))


def lengths_of(r, m):
    first = r.lens[m, 0:1, 0:1].astype(jnp.int32)
    return first, first + r.lens[m, 0:1, 1:2].astype(jnp.int32)


def tables(r, m):
    first_end, last_end = lengths_of(r, m)
    lane, slot = lanes(), slots()
    inverse = jnp.exp((lane % 32).astype(F32) * (-2.0 * math.log(BASE) / HD))
    position = slot - jnp.where(slot >= first_end, first_end, 0)
    position = position - jnp.where(slot >= last_end, last_end - first_end, 0)
    angle = position.astype(F32) * inverse
    sine = jnp.sin(angle)
    r.cs[m] = jnp.cos(angle)
    r.sn[m] = jnp.where(lane % 64 < 32, -sine, sine)


def side_rows(wq, wk, wv, gain_one, gain_two):
    lane = lax.broadcasted_iota(jnp.int32, (OWN, 128), 1)
    none = jnp.zeros((OWN, 64), F32)
    tail = jnp.concatenate([wq[:, 512:576].astype(F32), none], axis=1)
    key_a = pltpu.roll(wk[:, :128].astype(F32), 64, 1)
    key_b = pltpu.roll(jnp.concatenate([wk[:, 128:192].astype(F32), none], axis=1), 64, 1)
    last = jnp.concatenate([wv[:, 128:192].astype(F32), none], axis=1)
    row = lax.broadcasted_iota(jnp.int32, (128, OWN), 0)
    gains = jnp.where(
        row == 64, gain_one[...].astype(F32), jnp.where(row == 65, gain_two[...].astype(F32), 0.0)
    ).T
    return {
        512: jnp.where(lane < 64, tail, key_a),
        640: jnp.where(lane < 64, key_a, key_b),
        768: wv[:, :128].astype(F32),
        896: last + gains,
    }


def forward(r, m, arrived):
    x = r.x[m]
    n1 = x * norm_scale(x)
    wq, wo, wg, wu, wd = r.wq, r.wo, r.wg, r.wu, r.wd
    g1, g2 = r.gains[0:1, :], r.gains[1:2, :]
    entry = (n1 * g1).astype(BF16)
    r.ent[m] = entry
    qkv = dot(entry, wq[...])
    lane = lanes()
    cosine, sine = r.cs[m], r.sn[m]
    first_end, last_end = lengths_of(r, m)
    allowed = (
        segment_of(slots(), first_end, last_end) == segment_of(lane, first_end, last_end)
    ) & (lane <= slots())
    allowed = jnp.concatenate([allowed.astype(F32)] * 3, axis=0) > 0.5
    blocks = []
    for b in range(6):
        u = qkv[:, 128 * b : 128 * b + 128]
        blocks.append(u * cosine + turned(u, lane) * sine)
    groups = range(3)
    keys = [both_halves(blocks[(9 + g) // 2], (9 + g) % 2, lane).astype(BF16) for g in groups]
    values = [
        both_halves(qkv[:, 768 + 128 * (g // 2) : 896 + 128 * (g // 2)], g % 2, lane).astype(BF16)
        for g in groups
    ]
    queries = [
        jnp.concatenate(
            [
                jnp.where(lane // 64 == j % 2, blocks[j // 2], 0.0).astype(BF16)
                for j in range(3 * g, 3 * g + 3)
            ],
            axis=0,
        )
        for g in groups
    ]
    scores = [
        jnp.where(allowed, dot_nt(q, k) * HD**-0.5, -1e30) for q, k in zip(queries, keys)
    ]
    tops = [jnp.max(v, axis=-1, keepdims=True) for v in scores]
    weights = [jnp.exp(v - top) for v, top in zip(scores, tops)]
    sums = [jnp.sum(w, axis=-1, keepdims=True) for w in weights]
    probs = [w / total for w, total in zip(weights, sums)]
    outs = [dot(p.astype(BF16), v) for p, v in zip(probs, values)]
    heads = [out[ROWS * j : ROWS * (j + 1)] for out in outs for j in range(3)]
    for g in groups:
        r.kd[m, g] = keys[g]
        r.vd[m, g] = values[g]
        r.qs[m, g] = queries[g]
        r.pr[m, g] = probs[g]
    for b in range(4):
        r.mix[m, :, 128 * b : 128 * b + 128] = jnp.where(
            lane < 64, heads[2 * b], heads[2 * b + 1]
        ).astype(BF16)
    r.mix[m, :, 512:576] = heads[8][:, :64].astype(BF16)
    arrived("wo")
    middle = x + dot(r.mix[m], wo[...])
    r.mid[m] = middle
    second = (middle * norm_scale(middle) * g2).astype(BF16)
    r.sec[m] = second
    for j in range(0, FF, 256):
        cols = slice(j, j + 256)
        if j % (FF // 2) == 0:
            arrived("wg" + str(j))
            arrived("wu" + str(j))
        gate = dot(second, wg[:, cols])
        up = dot(second, wu[:, cols])
        sig = 1.0 / (1.0 + jnp.exp(-gate))
        swish = gate * sig
        r.inn[m, :, cols] = (swish * up).astype(BF16)
        r.fa[m, :, cols] = up * sig * (1.0 + gate * (1.0 - sig))
        r.fb[m, :, cols] = swish
    arrived("wd")
    return middle + dot_nt(r.inn[m], wd[...])


def backward(r, m, halfway):
    wq, wo, wg, wu, wd = r.wq, r.wo, r.wg, r.wu, r.wd
    g1, g2 = r.gains[0:1, :], r.gains[1:2, :]
    dy = r.dy[m]
    middle = r.mid[m]
    scale_two = norm_scale(middle)
    n2 = middle * scale_two
    df = dy.astype(BF16)
    r.df[m] = df
    for j in range(0, FF, 256):
        cols = slice(j, j + 256)
        d_inner = dot(df, wd[:, cols])
        r.dg[m, :, cols] = (d_inner * r.fa[m, :, cols]).astype(BF16)
        r.du[m, :, cols] = (d_inner * r.fb[m, :, cols]).astype(BF16)
    halfway()
    d_second = dot_nt(r.dg[m], wg[...]) + dot_nt(r.du[m], wu[...])
    r.gsum[m, 1:2, :] = jnp.sum(d_second * n2, axis=0, keepdims=True)
    d_middle = dy + norm_back(d_second * g2, n2, scale_two)
    branch = d_middle.astype(BF16)
    r.db[m] = branch
    d_mixed = dot_nt(branch, wo[...])
    lane = lanes()
    cosine, sine = r.cs[m], r.sn[m]
    groups = range(3)
    uppers = []
    for g in groups:
        parts = []
        for j in range(3 * g, 3 * g + 3):
            if j < 8:
                block = d_mixed[:, 128 * (j // 2) : 128 * (j // 2) + 128]
                block = jnp.where(lane // 64 == j % 2, block, 0.0)
            else:
                block = jnp.concatenate([d_mixed[:, 512:576], jnp.zeros((ROWS, 64), F32)], axis=1)
            parts.append(block.astype(BF16))
        uppers.append(jnp.concatenate(parts, axis=0))
    probs = [r.pr[m, g] for g in groups]
    d_probs = [dot_nt(uppers[g], r.vd[m, g]) for g in groups]
    dv = [dot_tn(probs[g].astype(BF16), uppers[g]) for g in groups]
    totals = [jnp.sum(d_probs[g] * probs[g], axis=-1, keepdims=True) for g in groups]
    d_scores = [
        (probs[g] * (d_probs[g] - totals[g]) * HD**-0.5).astype(BF16) for g in groups
    ]
    queries = [dot(d_scores[g], r.kd[m, g]) for g in groups]
    dk = [dot_tn(d_scores[g], r.qs[m, g]) for g in groups]
    dq = [q[ROWS * j : ROWS * (j + 1)] for q in queries for j in range(3)]
    dk = [key + pltpu.roll(key, 64, 1) for key in dk]
    dv = [value + pltpu.roll(value, 64, 1) for value in dv]
    heads = dq + dk
    for b in range(6):
        u = jnp.where(lane < 64, heads[2 * b], heads[2 * b + 1])
        r.dqkv[m, :, 128 * b : 128 * b + 128] = (u * cosine - turned(u, lane) * sine).astype(
            BF16
        )
    r.dqkv[m, :, 768:896] = jnp.where(lane < 64, dv[0], dv[1]).astype(BF16)
    r.dqkv[m, :, 896:1024] = jnp.where(lane < 64, dv[2], 0.0).astype(BF16)
    d_entry = dot_nt(r.dqkv[m], wq[...])
    x = r.x[m]
    scale_one = norm_scale(x)
    n1 = x * scale_one
    r.gsum[m, 0:1, :] = jnp.sum(d_entry * n1, axis=0, keepdims=True)
    return d_middle + norm_back(d_entry * g1, n1, scale_one)


def whole(ref, cols=slice(None)):
    value = ref[:, :, cols]
    return value.reshape(M, value.shape[-1])


def store(flat, start, block):
    flat[0, start : start + OWN] = block[:OWN].astype(BF16)
    flat[1, start : start + OWN] = block[OWN:].astype(BF16)


def gate_grads(r, flat, done):
    second_t = whole(r.sec).T
    for ref, start in ((r.dg, GATE), (r.du, UP)):
        for b in range(0, 12, 2):
            g = dot(second_t, whole(ref, slice(128 * b, 128 * b + 256)))
            store(flat, start + b * OWN, g[:, :128])
            store(flat, start + (b + 1) * OWN, g[:, 128:])
            done(start + (b + 2) * OWN)


def down_grads(r, flat, done):
    df_t = whole(r.df).T
    for b in range(6):
        for owner in range(2):
            first = 768 * owner + 128 * b
            g = dot(df_t, whole(r.inn, slice(first, first + 128)))
            flat[owner, DOWN + b * D : DOWN + (b + 1) * D] = g.astype(BF16)
        done(DOWN + (b + 1) * D)


def rest_grads(r, flat, done):
    entry_t = whole(r.ent).T
    mixed_t = whole(r.mix).T
    for b in range(0, 8, 2):
        g = dot(entry_t, whole(r.dqkv, slice(128 * b, 128 * b + 256)))
        store(flat, QKV + b * OWN, g[:, :128])
        if b == 6:
            rest = whole(r.db, slice(512, 576)).astype(F32)
            rest = jnp.concatenate([rest, jnp.zeros((M, 64), F32)], axis=1)
            rest = pltpu.roll(rest, 64, 1).astype(BF16)
            store(flat, QKV + 7 * OWN, g[:, 128:] + dot(mixed_t, rest))
        else:
            store(flat, QKV + (b + 1) * OWN, g[:, 128:])
        done(QKV + (b + 2) * OWN)
    for b in range(0, 4, 2):
        g = dot(mixed_t, whole(r.db, slice(128 * b, 128 * b + 256)))
        store(flat, OUT + b * OWN, g[:, :128])
        store(flat, OUT + (b + 1) * OWN, g[:, 128:])
        done(OUT + (b + 2) * OWN)
    sums = r.gsum[0] + r.gsum[1]
    row = lax.broadcasted_iota(jnp.int32, (128, D), 0)
    store(flat, GAIN, jnp.where(row == 0, sums[0:1], jnp.where(row == 1, sums[1:2], 0.0)).T)
    flat[0, USED:] = jnp.zeros((FLAT - USED, 128), BF16)
    flat[1, USED:] = jnp.zeros((FLAT - USED, 128), BF16)
    done(FLAT)


KEPT = dict(
    wq=((D, 1024), BF16),
    wo=((D, D), BF16),
    wg=((D, FF), BF16),
    wu=((D, FF), BF16),
    wd=((D, FF), BF16),
    gains=((8, D), F32),
    x=((MICRO, ROWS, D), F32),
    dy=((MICRO, ROWS, D), F32),
    lens=((MICRO, 8, 128), F32),
    lens_own=((MICRO, 8, 128), F32),
    lens_pair=((MICRO, 8, 128), F32),
    cot_pair=((MICRO, D, ROWS), BF16),
    tok=((MICRO, D, ROWS), BF16),
    y_send=((MICRO, ROWS, D), BF16),
    y_box=((MICRO, ROWS, D), BF16),
    y_turn=((MICRO, D, ROWS), BF16),
    dx_send=((MICRO, ROWS, D), BF16),
    dx_box=((MICRO, ROWS, D), BF16),
    dx_turn=((MICRO, D, ROWS), BF16),
    ent=((MICRO, ROWS, D), BF16),
    qs=((MICRO, 3, 3 * ROWS, 128), BF16),
    kd=((MICRO, 3, ROWS, 128), BF16),
    vd=((MICRO, 3, ROWS, 128), BF16),
    pr=((MICRO, 3, 3 * ROWS, 128), F32),
    mix=((MICRO, ROWS, D), BF16),
    mid=((MICRO, ROWS, D), F32),
    sec=((MICRO, ROWS, D), BF16),
    inn=((MICRO, ROWS, FF), BF16),
    fa=((MICRO, ROWS, FF), F32),
    fb=((MICRO, ROWS, FF), F32),
    cs=((MICRO, ROWS, 128), F32),
    sn=((MICRO, ROWS, 128), F32),
    df=((MICRO, ROWS, D), BF16),
    dg=((MICRO, ROWS, FF), BF16),
    du=((MICRO, ROWS, FF), BF16),
    db=((MICRO, ROWS, D), BF16),
    dqkv=((MICRO, ROWS, 1024), BF16),
    gsum=((MICRO, 8, D), F32),
    flat=((2, FLAT, 128), BF16),
    cross=((FLAT, 128), BF16),
    one=((6 * PARTS, max(SIZE) // 8, 128), BF16),
    two=((7 * PARTS, max(SIZE) // 32, 128), BF16),
    o=((FLAT, 128), BF16),
)
SEMS = dict(
    w=7,
    swap=2,
    y=2,
    dx=2,
    y_swap=2,
    dx_swap=2,
    cross=4 * PARTS,
    one=6 * PARTS,
    two=7 * PARTS,
    along=7 * PARTS,
    back=12 * PARTS,
)


def vmem(n):
    return [pl.BlockSpec(memory_space=pltpu.VMEM)] * n


def hbm(n):
    return [pl.BlockSpec(memory_space=pl.ANY)] * n


PLANE = [(0, 1), (1, 0), (3, 0), (1, 1), (3, 1), (2, 0), (2, 1)]


def places():
    section, core, replica = (lax.axis_index(a) for a in ("section", "shard", "replica"))
    x, y, z = replica // 8, replica // 2 % 4, replica % 2

    def at(x_, y_, z_):
        return (section, core, x_ * 8 + y_ * 2 + z_)

    return SimpleNamespace(
        section=section,
        core=core,
        x=x,
        y=y,
        z=z,
        x_next=at((x + 1) % 4, y, z),
        x_prev=at((x + 3) % 4, y, z),
        y_next=at(x, (y + 1) % 4, z),
        y_prev=at(x, (y + 3) % 4, z),
        z_pair=at(x, y, 1 - z),
        x_plane=[at((x + k) % 4, y, (z + w) % 2) for k, w in PLANE],
        y_plane=[at(x, (y + k) % 4, (z + w) % 2) for k, w in PLANE],
        partner=(section, 1 - core, replica),
        across=(1 - section, core, x * 8 + y * 2 + (1 - z)),
    )


def step_kernel(
    lens, tok, cot, gain_one, gain_two, wq_own, wk_own, wv_own, wo_own, wg_own, wu_own, wd_own,
    y_out, dx_out, o, *refs
):
    r = SimpleNamespace(**dict(zip(KEPT, refs)))
    sends = dict(zip(SEMS, refs[len(KEPT) :]))
    recvs = dict(zip(SEMS, refs[len(KEPT) + len(SEMS) :]))
    local = refs[len(KEPT) + 2 * len(SEMS)]
    at = places()
    section, core = at.section, at.core

    barrier = pltpu.get_barrier_semaphore()
    near = [at.partner, at.across, *at.x_plane, *at.y_plane[1:]]
    for device in near:
        pl.semaphore_signal(barrier, inc=1, device_id=device, device_id_type=MESH)
    def remote(name, i, src, dst, device):
        return pltpu.make_async_remote_copy(
            src,
            dst,
            sends[name].at[i],
            recvs[name].at[i],
            device_id=device,
            device_id_type=MESH,
        )

    tok_load = pltpu.make_async_copy(tok, r.tok, local.at[6])

    @pl.when(section == 0)
    def _():
        tok_load.start()

    own_rows = pl.ds(pl.multiple_of(core * OWN, 16), OWN)
    own_cols = pl.ds(pl.multiple_of(core * (FF // 2), 128), FF // 2)
    weight_places = {"wo": (wo_own, r.wo.at[own_rows])}
    for j in range(0, FF, FF // 2):
        cols = slice(j, j + FF // 2)
        weight_places["wg" + str(j)] = (wg_own.at[:, cols], r.wg.at[own_rows, cols])
        weight_places["wu" + str(j)] = (wu_own.at[:, cols], r.wu.at[own_rows, cols])
    weight_places["wd"] = (wd_own, r.wd.at[:, own_cols])
    side_place = r.wq.at[own_rows]
    weight_copies = {"side": [remote("w", 0, side_place, side_place, at.partner)]}
    for i, (name, (src, dst)) in enumerate(weight_places.items()):
        weight_copies[name] = [
            remote("w", i + 1, src, dst, at.partner),
            pltpu.make_async_copy(src, dst, local.at[i]),
        ]
        weight_copies[name][1].start()
    r.wq[own_rows, :512] = wq_own[:, :512]
    for start, value in side_rows(wq_own, wk_own, wv_own, gain_one, gain_two).items():
        r.wq[own_rows, start : start + 128] = value.astype(BF16)

    r.lens_own[...] = jnp.zeros((MICRO, 8, 128), F32)
    for m in range(MICRO):
        r.lens_own[m, 0:1, 0:2] = lens[m : m + 1, :].astype(F32)
    lens_swap = remote("swap", 0, r.lens_own, r.lens_pair, at.z_pair)
    cot_swap = remote("swap", 1, cot, r.cot_pair, at.z_pair)

    pl.semaphore_wait(barrier, len(near))
    for name in ("side", "wo"):
        weight_copies[name][0].start()
    lens_swap.start()
    cot_swap.start()

    @pl.when(section == 0)
    def _():
        r.lens[...] = r.lens_own[...]
        tok_load.wait()
        for m in range(MICRO):
            r.x[m] = r.tok[m].astype(F32).T

    @pl.when(section == 1)
    def _():
        lens_swap.wait_recv()
        r.lens[...] = r.lens_pair[...]

    for m in range(MICRO):
        tables(r, m)
    weight_copies["side"][0].wait_recv()
    for name in weight_places:
        if name != "wo":
            weight_copies[name][0].start()
    r.gains[...] = r.wq[:, 896:1024].astype(F32).T[64:72]

    def y_copy(m):
        return remote("y", m, r.y_send.at[m], r.y_box.at[m], at.across)

    def dx_copy(m):
        return remote("dx", m, r.dx_send.at[m], r.dx_box.at[m], at.across)

    def y_swap(m):
        return remote("y_swap", m, r.y_turn.at[m], y_out.at[m], at.z_pair)

    def y_store(m):
        return pltpu.make_async_copy(r.y_turn.at[m], y_out.at[m], local.at[6 + m])

    def dx_store(m):
        return pltpu.make_async_copy(r.dx_turn.at[m], dx_out.at[m], local.at[8 + m])

    def dx_swap(m):
        return remote("dx_swap", m, r.dx_turn.at[m], dx_out.at[m], at.z_pair)

    total = Total(r, at, remote)

    def tick(t, carry):
        m = jnp.where(section == 0, t % 2, t // 2)
        ahead = jnp.where(section == 0, t // 2, t % 2) == 0

        @pl.when(ahead)
        def _():
            @pl.when(section == 1)
            def _():
                y_copy(m).wait_recv()
                r.x[m] = r.y_box[m].astype(F32)

            def arrived(name):
                @pl.when(t == 0)
                def _():
                    for i, copy in enumerate(weight_copies[name]):
                        if i == 0:
                            copy.wait_recv()
                        else:
                            copy.wait()

            y = forward(r, m, arrived)
            r.y_send[m] = y.astype(BF16)

            @pl.when(section == 0)
            def _():
                y_copy(m).start()
                r.y_turn[m] = r.y_send[m].astype(F32).T.astype(BF16)
                y_store(m).start()

            @pl.when(section == 1)
            def _():
                r.y_turn[m] = r.y_send[m].astype(F32).T.astype(BF16)
                y_swap(m).start()

        @pl.when(jnp.logical_not(ahead))
        def _():
            @pl.when(section == 0)
            def _():
                dx_copy(m).wait_recv()
                r.dy[m] = r.dx_box[m].astype(F32)

            @pl.when(section == 1)
            def _():
                @pl.when(t == 1)
                def _():
                    cot_swap.wait_recv()

                ids = lax.broadcasted_iota(jnp.int32, (ROWS, D), 0)
                live = ids < lengths_of(r, m)[1]
                r.dy[m] = jnp.where(live, r.cot_pair[m].astype(F32).T, 0.0)

            def halfway():
                @pl.when(jnp.logical_and(section == 0, t == 2 * MICRO - 1))
                def _():
                    gate_grads(r, r.flat, total.starter())

            r.dx_send[m] = backward(r, m, halfway).astype(BF16)

            @pl.when(section == 0)
            def _():
                r.dx_turn[m] = r.dx_send[m].astype(F32).T.astype(BF16)
                dx_store(m).start()

            @pl.when(section == 1)
            def _():
                dx_copy(m).start()
                r.dx_turn[m] = r.dx_send[m].astype(F32).T.astype(BF16)
                dx_swap(m).start()

        return carry

    lax.fori_loop(0, 2 * MICRO, tick, 0)

    @pl.when(section == 0)
    def _():
        lens_swap.wait_recv()
        cot_swap.wait_recv()

    @pl.when(section == 1)
    def _():
        gate_grads(r, r.flat, total.starter())

    started = total.starter(DOWN)
    total.step_1(0)
    down_grads(r, r.flat, started)
    rest_grads(r, r.flat, started)
    total.run(o, local)
    total.finish()

    lens_swap.wait_send()
    cot_swap.wait_send()
    for copies in weight_copies.values():
        copies[0].wait_send()

    @pl.when(section == 0)
    def _():
        for m in range(MICRO):
            y_copy(m).wait_send()
            y_store(m).wait()
            dx_store(m).wait()

    @pl.when(section == 1)
    def _():
        for m in range(MICRO):
            dx_copy(m).wait_send()
            y_swap(m).wait()
            dx_swap(m).wait()


def span(start, count):
    return pl.ds(pl.multiple_of(start, 16), count)


class Total:
    def __init__(self, r, at, remote):
        self.flat, self.box, self.one, self.two, self.o = r.flat, r.cross, r.one, r.two, r.o
        self.at, self.remote = at, remote
        self.core = at.core
        self.pos = ((at.x, at.y), (at.y, at.x))
        xs, ys = (at.x_next, at.x_prev), (at.y_next, at.y_prev)
        self.first = (xs, ys)
        self.plane = (at.y_plane, at.x_plane)
        self.sent = []
        self.copies = {}

    def send(self, name, i, src, dst, device):
        copy = self.remote(name, i, src, dst, device)
        copy.start()
        self.sent.append(copy)
        self.copies[name, i] = copy

    def got(self, name, i):
        self.copies[name, i].wait_recv()

    def cross(self, n):
        i, q = n // 4, n % 4
        count = SIZE[i] // 4
        rows = slice(BASE_ROW[i] + q * count, BASE_ROW[i] + (q + 1) * count)
        src = self.flat.at[1 - self.core, rows]
        return self.remote("cross", n, src, self.box.at[rows], self.at.partner)

    def starter(self, first=0):
        ends = [BASE_ROW[n // 4] + (n % 4 + 1) * SIZE[n // 4] // 4 for n in range(4 * PARTS)]
        begun = [sum(end <= first for end in ends)]

        def ready(rows):
            while begun[0] < len(ends) and ends[begun[0]] <= rows:
                self.cross(begun[0]).start()
                begun[0] += 1

        return ready

    def rows(self, i, k, start=0, count=None):
        place = SIZE[i] // 4 * ((self.pos[i % 2][0] + k) % 4)
        return span(BASE_ROW[i] + place + start, count)

    def piece(self, i, k):
        return SIZE[i] // 16 * ((self.pos[i % 2][1] + k) % 4)

    def add(self, i, k, upper, *others):
        count = SIZE[i] // 8
        rows = self.rows(i, k, upper * count, count)
        value = self.flat[self.core, rows].astype(F32) + self.box[rows].astype(F32)
        for other in others:
            value = value + other.astype(F32)
        self.flat[self.core, rows] = value.astype(BF16)
        return self.flat.at[self.core, rows]

    def go(self, i, slot, ref, way):
        device = self.first[i % 2][way]
        box = self.one.at[i * 6 + slot, : SIZE[i] // 8]
        self.send("one", i * 6 + slot, ref, box, device)

    def box_of(self, i, slot):
        self.got("one", i * 6 + slot)
        return self.one[i * 6 + slot, : SIZE[i] // 8]

    def step_1(self, c):
        for i in (2 * c, 2 * c + 1):
            for q in range(4):
                self.cross(i * 4 + q).wait_recv()
            self.go(i, 0, self.add(i, 2, 0), 0)
            self.go(i, 1, self.add(i, 2, 1), 1)
        for i in (2 * c, 2 * c + 1):
            self.go(i, 2, self.add(i, 1, 1), 0)
            self.go(i, 3, self.add(i, 3, 0), 1)

    def step_2(self, c):
        for i in (2 * c, 2 * c + 1):
            self.go(i, 4, self.add(i, 1, 0, self.box_of(i, 0)), 0)
            self.go(i, 5, self.add(i, 3, 1, self.box_of(i, 1)), 1)

    def block(self, i, k, w):
        count = SIZE[i] // 32
        return self.rows(i, 0, self.piece(i, k) + count * ((self.at.z + w) % 2), count)

    def two_box(self, i, j):
        return self.two.at[i * 7 + j, : SIZE[i] // 32]

    def step_3(self, c):
        for i in (2 * c, 2 * c + 1):
            self.add(i, 0, 0, self.box_of(i, 3), self.box_of(i, 4))
            self.add(i, 0, 1, self.box_of(i, 2), self.box_of(i, 5))
            for j, (k, w) in enumerate(PLANE):
                src = self.flat.at[self.core, self.block(i, k, w)]
                self.send("two", i * 7 + j, src, self.two_box(i, j), self.plane[i % 2][j])

    def step_4(self, c):
        for i in (2 * c, 2 * c + 1):
            rows = self.block(i, 0, 0)
            value = self.flat[self.core, rows].astype(F32)
            for j in range(7):
                self.got("two", i * 7 + j)
                value = value + self.two[i * 7 + j, : SIZE[i] // 32].astype(F32)
            self.o[rows] = value.astype(BF16)
            ref = self.o.at[rows]
            for j in range(7):
                self.send("along", i * 7 + j, ref, ref, self.plane[i % 2][j])

    def unit(self, i, k1, k2):
        return self.o.at[self.rows(i, k1, self.piece(i, k2), SIZE[i] // 16)]

    def step_5(self, c):
        for k in (0, 1, 3, 2):
            for i in (2 * c, 2 * c + 1):
                for j, (there, _) in enumerate(PLANE):
                    if there == k:
                        self.got("along", i * 7 + j)
                back = (4 - k) % 4
                ref = self.unit(i, 0, back)
                for d in range(2):
                    self.send("back", i * 12 + d * 6 + back, ref, ref, self.first[i % 2][d])

    def step_6(self, c):
        for k in (0, 3, 1, 2):
            for i in (2 * c, 2 * c + 1):
                self.got("back", i * 12 + k)
                self.got("back", i * 12 + 6 + k)
                way = 0 if k in (0, 3) else 1
                ref = self.unit(i, 1 if way else 3, k)
                slot = i * 12 + way * 6 + (4 if k < 2 else 5)
                self.send("back", slot, ref, ref, self.first[i % 2][way])

    def step_7(self, c):
        for i in (2 * c, 2 * c + 1):
            for slot in (4, 5, 10, 11):
                self.got("back", i * 12 + slot)
        rows = slice(BASE_ROW[2 * c], BASE_ROW[2 * c] + CHUNKS[c])
        copy = pltpu.make_async_copy(self.o.at[rows], self.out.at[rows], self.sem.at[c])
        copy.start()
        self.written.append(copy)

    def run(self, out, sem):
        self.out, self.sem, self.written = out, sem, []
        for n in range(2, 7 + len(CHUNKS)):
            for c in range(len(CHUNKS)):
                if 1 <= n - c <= 7:
                    getattr(self, f"step_{n - c}")(c)
        for copy in self.written:
            copy.wait()

    def finish(self):
        for n in range(4 * PARTS):
            self.cross(n).wait_send()
        for copy in self.sent:
            copy.wait_send()


def run_step(lens, tok, cot, gain_one, gain_two, wq, wk, wv, wo, wg, wu, wd):
    rows = jax.ShapeDtypeStruct((MICRO, D, ROWS), BF16)
    sems = [pltpu.SemaphoreType.DMA((n,)) for n in SEMS.values()]
    return pl.pallas_call(
        step_kernel,
        out_shape=[rows, rows, jax.ShapeDtypeStruct((FLAT, 128), BF16)],
        in_specs=vmem(1) + hbm(2) + vmem(5) + hbm(4),
        out_specs=hbm(3),
        scratch_shapes=[pltpu.VMEM(*v) for v in KEPT.values()]
        + sems
        + sems
        + [pltpu.SemaphoreType.DMA((10,))],
        compiler_params=pltpu.CompilerParams(
            collective_id=1, has_side_effects=True, vmem_limit_bytes=VMEM_LIMIT
        ),
    )(lens, tok, cot, gain_one, gain_two, wq, wk, wv, wo, wg, wu, wd)


def unpack_kernel(
    f, y, dx, y_out, dx_out, gain_one, wq, wk, wv, wo, gain_two, wg, wu, wd, *refs
):
    flat, s_y, s_dx, s_wq, s_wk, s_wv, s_wo, s_wg, s_wu, s_wd, arrive, leave = refs
    step = 6 * OWN
    bounds = (*range(0, QKV, step), QKV, USED)
    loads = []

    def load(src, dst):
        loads.append(pltpu.make_async_copy(src, dst, arrive.at[len(loads)]))
        loads[-1].start()

    for i in range(len(bounds) - 1):
        part = slice(bounds[i], bounds[i + 1])
        load(f.at[part], flat.at[part])
    load(y, s_y)
    load(dx, s_dx)
    stores = []

    def put(src, dst):
        stores.append(pltpu.make_async_copy(src, dst, leave.at[len(stores)]))
        stores[-1].start()

    def rows(start, count=OWN):
        return flat[start : start + count].astype(F32)

    n = 0
    for start, stage, dst in ((GATE, s_wg, wg), (UP, s_wu, wu)):
        for j in range(0, 12, 6):
            loads[n].wait()
            n += 1
            for b in range(j, j + 6):
                stage[:, 128 * b : 128 * b + 128] = rows(start + b * OWN)
            cols = slice(128 * j, 128 * j + 768)
            put(stage.at[:, cols], dst.at[0, :, cols])
    for j in range(0, 6, 3):
        loads[n].wait()
        n += 1
        for b in range(j, j + 3):
            s_wd[:, 128 * b : 128 * b + 128] = rows(DOWN + b * D, D)
        cols = slice(128 * j, 128 * j + 384)
        put(s_wd.at[:, cols], wd.at[0, :, cols])
    loads[n].wait()
    n += 1
    swap = [pltpu.roll(rows(QKV + b * OWN), 64, 1) for b in range(4, 8)]
    lane = lax.broadcasted_iota(jnp.int32, (OWN, 128), 1)
    for b in range(4):
        s_wq[:, 128 * b : 128 * b + 128] = rows(QKV + b * OWN)
        s_wo[:, 128 * b : 128 * b + 128] = rows(OUT + b * OWN)
    s_wq[:, 512:576] = rows(QKV + 4 * OWN)[:, :64]
    put(s_wq, wq.at[0])
    s_wo[:, 512:576] = swap[3][:, :64]
    put(s_wo, wo.at[0])
    s_wk[:, :128] = jnp.where(lane < 64, swap[0], swap[1])
    s_wk[:, 128:] = swap[1][:, :64]
    put(s_wk, wk.at[0])
    s_wv[:, :128] = rows(QKV + 6 * OWN)
    s_wv[:, 128:] = rows(QKV + 7 * OWN)[:, :64]
    put(s_wv, wv.at[0])
    for src, dst in ((s_y, y_out), (s_dx, dx_out)):
        loads[n].wait()
        n += 1
        put(src, dst)
    gains = rows(GAIN).T
    gain_one[...] = gains[0:1]
    gain_two[...] = gains[1:2]
    for copy in stores:
        copy.wait()


def run_unpack(flat, y, dx):
    kinds = [(1, OWN), (1, OWN, D), (1, OWN, 192), (1, OWN, 192), (1, OWN, D)]
    kinds += [(1, OWN), (1, OWN, FF), (1, OWN, FF), (1, D, FF // 2)]
    stages = [pltpu.VMEM(k[1:], F32) for k in kinds if len(k) == 3]
    return pl.pallas_call(
        unpack_kernel,
        out_shape=[jax.ShapeDtypeStruct(a.shape, a.dtype) for a in (y, dx)]
        + [jax.ShapeDtypeStruct(k, F32) for k in kinds],
        in_specs=hbm(3),
        out_specs=hbm(2) + [(vmem if len(k) == 2 else hbm)(1)[0] for k in kinds],
        scratch_shapes=[pltpu.VMEM((FLAT, 128), BF16)]
        + [pltpu.VMEM(y.shape, y.dtype)] * 2
        + stages
        + [pltpu.SemaphoreType.DMA((9,)), pltpu.SemaphoreType.DMA((12,))],
        compiler_params=pltpu.CompilerParams(vmem_limit_bytes=VMEM_LIMIT),
    )(flat, y, dx)


def shards(
    tokens,
    cotangent,
    seq_lengths,
    gain_attn,
    w_query,
    w_key,
    w_value,
    w_out,
    gain_ffn,
    w_gate,
    w_up,
    w_down,
):
    y, dx, flat = run_step(
        seq_lengths,
        jnp.swapaxes(tokens, 1, 2),
        jnp.swapaxes(cotangent, 1, 2),
        gain_attn,
        gain_ffn,
        w_query[0],
        w_key[0],
        w_value[0],
        w_out[0],
        w_gate[0],
        w_up[0],
        w_down[0].T,
    )
    y, dx, *grads = run_unpack(flat, y, dx)
    grads[8] = jnp.swapaxes(grads[8], 1, 2)
    return (jnp.swapaxes(y, 1, 2)[None], jnp.swapaxes(dx, 1, 2)[None], *grads)


def solution(mesh):
    row_spec = P(None, ("shard", "replica"), None)
    out_spec = P("section", None, ("shard", "replica"), None)
    vector = P("section", "shard")
    matrix = P("section", "shard", None)
    weight_specs = (vector, matrix, matrix, matrix, matrix, vector, matrix, matrix, matrix)
    return jax.shard_map(
        shards,
        mesh=mesh,
        in_specs=(row_spec, row_spec, P(None, ("shard", "replica")), *weight_specs),
        out_specs=(out_spec, out_spec, *weight_specs),
        check_vma=False,
    )
```

```python
import functools
import math
from types import SimpleNamespace

import jax
import jax.numpy as jnp
from jax import lax
from jax.experimental import pallas as pl
from jax.experimental.pallas import tpu as pltpu
from jax.sharding import PartitionSpec as P

MESH = pl.DeviceIdType.MESH
F32 = jnp.float32
BF16 = jnp.bfloat16

D = 576
HD = 64
FF = 1536
ROWS = 128
MICRO = 2
M = MICRO * ROWS
OWN = D // 2
EPS = 1e-05
BASE = 100000.0
VMEM_LIMIT = 62 * 1024 * 1024

GATE = 0
UP = GATE + 12 * OWN
DOWN = UP + 12 * OWN
QKV = DOWN + 6 * D
OUT = QKV + 8 * OWN
GAIN = OUT + 4 * OWN
USED = GAIN + OWN
FLAT = 14336
CHUNKS = (5120, 5120, 4096)
PARTS = 2 * len(CHUNKS)
SIZE = [n // 2 for n in CHUNKS for _ in range(2)]
BASE_ROW = [sum(SIZE[:i]) for i in range(PARTS)]


def dot(a, b):
    return lax.dot_general(a, b, (((1,), (0,)), ((), ())), preferred_element_type=F32)


def dot_nt(a, b):
    return lax.dot_general(a, b, (((1,), (1,)), ((), ())), preferred_element_type=F32)


def dot_tn(a, b):
    return lax.dot_general(a, b, (((0,), (0,)), ((), ())), preferred_element_type=F32)


def lanes():
    return lax.broadcasted_iota(jnp.int32, (ROWS, 128), 1)


def slots():
    return lax.broadcasted_iota(jnp.int32, (ROWS, 128), 0)


def segment_of(ids, first_end, last_end):
    return jnp.where(ids >= first_end, 1, 0) + jnp.where(ids >= last_end, 1, 0)


def turned(u, lane):
    return jnp.where(lane % 64 < 32, pltpu.roll(u, 96, 1), pltpu.roll(u, 32, 1))


def both_halves(u, half, lane):
    return jnp.where(lane // 64 == half, u, pltpu.roll(u, 64, 1))


def norm_scale(x):
    return lax.rsqrt(jnp.mean(x * x, axis=-1, keepdims=True) + EPS)


def norm_back(upper, normed, scale):
    return scale * (upper - normed * jnp.mean(upper * normed, axis=-1, keepdims=True))


def lengths_of(r, m):
    first = r.lens[m, 0:1, 0:1].astype(jnp.int32)
    return first, first + r.lens[m, 0:1, 1:2].astype(jnp.int32)


def tables(r, m):
    first_end, last_end = lengths_of(r, m)
    lane, slot = lanes(), slots()
    inverse = jnp.exp((lane % 32).astype(F32) * (-2.0 * math.log(BASE) / HD))
    position = slot - jnp.where(slot >= first_end, first_end, 0)
    position = position - jnp.where(slot >= last_end, last_end - first_end, 0)
    angle = position.astype(F32) * inverse
    sine = jnp.sin(angle)
    r.cs[m] = jnp.cos(angle)
    r.sn[m] = jnp.where(lane % 64 < 32, -sine, sine)


def side_rows(wq, wk, wv, gain_one, gain_two):
    lane = lax.broadcasted_iota(jnp.int32, (OWN, 128), 1)
    none = jnp.zeros((OWN, 64), F32)
    tail = jnp.concatenate([wq[:, 512:576].astype(F32), none], axis=1)
    key_a = pltpu.roll(wk[:, :128].astype(F32), 64, 1)
    key_b = pltpu.roll(jnp.concatenate([wk[:, 128:192].astype(F32), none], axis=1), 64, 1)
    last = jnp.concatenate([wv[:, 128:192].astype(F32), none], axis=1)
    row = lax.broadcasted_iota(jnp.int32, (128, OWN), 0)
    gains = jnp.where(
        row == 64, gain_one[...].astype(F32), jnp.where(row == 65, gain_two[...].astype(F32), 0.0)
    ).T
    return {
        512: jnp.where(lane < 64, tail, key_a),
        640: jnp.where(lane < 64, key_a, key_b),
        768: wv[:, :128].astype(F32),
        896: last + gains,
    }


def forward(r, m, arrived):
    x = r.x[m]
    n1 = x * norm_scale(x)
    wq, wo, wg, wu, wd = r.wq, r.wo, r.wg, r.wu, r.wd
    g1, g2 = r.gains[0:1, :], r.gains[1:2, :]
    entry = (n1 * g1).astype(BF16)
    r.ent[m] = entry
    qkv = dot(entry, wq[...])
    lane = lanes()
    cosine, sine = r.cs[m], r.sn[m]
    first_end, last_end = lengths_of(r, m)
    allowed = (
        segment_of(slots(), first_end, last_end) == segment_of(lane, first_end, last_end)
    ) & (lane <= slots())
    allowed = jnp.concatenate([allowed.astype(F32)] * 3, axis=0) > 0.5
    blocks = []
    for b in range(6):
        u = qkv[:, 128 * b : 128 * b + 128]
        blocks.append(u * cosine + turned(u, lane) * sine)
    groups = range(3)
    keys = [both_halves(blocks[(9 + g) // 2], (9 + g) % 2, lane).astype(BF16) for g in groups]
    values = [
        both_halves(qkv[:, 768 + 128 * (g // 2) : 896 + 128 * (g // 2)], g % 2, lane).astype(BF16)
        for g in groups
    ]
    queries = [
        jnp.concatenate(
            [
                jnp.where(lane // 64 == j % 2, blocks[j // 2], 0.0).astype(BF16)
                for j in range(3 * g, 3 * g + 3)
            ],
            axis=0,
        )
        for g in groups
    ]
    scores = [
        jnp.where(allowed, dot_nt(q, k) * HD**-0.5, -1e30) for q, k in zip(queries, keys)
    ]
    tops = [jnp.max(v, axis=-1, keepdims=True) for v in scores]
    weights = [jnp.exp(v - top) for v, top in zip(scores, tops)]
    sums = [jnp.sum(w, axis=-1, keepdims=True) for w in weights]
    probs = [w / total for w, total in zip(weights, sums)]
    outs = [dot(p.astype(BF16), v) for p, v in zip(probs, values)]
    heads = [out[ROWS * j : ROWS * (j + 1)] for out in outs for j in range(3)]
    for g in groups:
        r.kd[m, g] = keys[g]
        r.vd[m, g] = values[g]
        r.qs[m, g] = queries[g]
        r.pr[m, g] = probs[g]
    for b in range(4):
        r.mix[m, :, 128 * b : 128 * b + 128] = jnp.where(
            lane < 64, heads[2 * b], heads[2 * b + 1]
        ).astype(BF16)
    r.mix[m, :, 512:576] = heads[8][:, :64].astype(BF16)
    arrived("wo")
    middle = x + dot(r.mix[m], wo[...])
    r.mid[m] = middle
    second = (middle * norm_scale(middle) * g2).astype(BF16)
    r.sec[m] = second
    for j in range(0, FF, 256):
        cols = slice(j, j + 256)
        if j % (FF // 2) == 0:
            arrived("wg" + str(j))
            arrived("wu" + str(j))
        gate = dot(second, wg[:, cols])
        up = dot(second, wu[:, cols])
        sig = 1.0 / (1.0 + jnp.exp(-gate))
        swish = gate * sig
        r.inn[m, :, cols] = (swish * up).astype(BF16)
        r.fa[m, :, cols] = up * sig * (1.0 + gate * (1.0 - sig))
        r.fb[m, :, cols] = swish
    arrived("wd")
    return middle + dot_nt(r.inn[m], wd[...])


def backward(r, m, halfway):
    wq, wo, wg, wu, wd = r.wq, r.wo, r.wg, r.wu, r.wd
    g1, g2 = r.gains[0:1, :], r.gains[1:2, :]
    dy = r.dy[m]
    middle = r.mid[m]
    scale_two = norm_scale(middle)
    n2 = middle * scale_two
    df = dy.astype(BF16)
    r.df[m] = df
    for j in range(0, FF, 256):
        cols = slice(j, j + 256)
        d_inner = dot(df, wd[:, cols])
        r.dg[m, :, cols] = (d_inner * r.fa[m, :, cols]).astype(BF16)
        r.du[m, :, cols] = (d_inner * r.fb[m, :, cols]).astype(BF16)
    halfway()
    d_second = dot_nt(r.dg[m], wg[...]) + dot_nt(r.du[m], wu[...])
    r.gsum[m, 1:2, :] = jnp.sum(d_second * n2, axis=0, keepdims=True)
    d_middle = dy + norm_back(d_second * g2, n2, scale_two)
    branch = d_middle.astype(BF16)
    r.db[m] = branch
    d_mixed = dot_nt(branch, wo[...])
    lane = lanes()
    cosine, sine = r.cs[m], r.sn[m]
    groups = range(3)
    uppers = []
    for g in groups:
        parts = []
        for j in range(3 * g, 3 * g + 3):
            if j < 8:
                block = d_mixed[:, 128 * (j // 2) : 128 * (j // 2) + 128]
                block = jnp.where(lane // 64 == j % 2, block, 0.0)
            else:
                block = jnp.concatenate([d_mixed[:, 512:576], jnp.zeros((ROWS, 64), F32)], axis=1)
            parts.append(block.astype(BF16))
        uppers.append(jnp.concatenate(parts, axis=0))
    probs = [r.pr[m, g] for g in groups]
    d_probs = [dot_nt(uppers[g], r.vd[m, g]) for g in groups]
    dv = [dot_tn(probs[g].astype(BF16), uppers[g]) for g in groups]
    totals = [jnp.sum(d_probs[g] * probs[g], axis=-1, keepdims=True) for g in groups]
    d_scores = [
        (probs[g] * (d_probs[g] - totals[g]) * HD**-0.5).astype(BF16) for g in groups
    ]
    queries = [dot(d_scores[g], r.kd[m, g]) for g in groups]
    dk = [dot_tn(d_scores[g], r.qs[m, g]) for g in groups]
    dq = [q[ROWS * j : ROWS * (j + 1)] for q in queries for j in range(3)]
    dk = [key + pltpu.roll(key, 64, 1) for key in dk]
    dv = [value + pltpu.roll(value, 64, 1) for value in dv]
    heads = dq + dk
    for b in range(6):
        u = jnp.where(lane < 64, heads[2 * b], heads[2 * b + 1])
        r.dqkv[m, :, 128 * b : 128 * b + 128] = (u * cosine - turned(u, lane) * sine).astype(
            BF16
        )
    r.dqkv[m, :, 768:896] = jnp.where(lane < 64, dv[0], dv[1]).astype(BF16)
    r.dqkv[m, :, 896:1024] = jnp.where(lane < 64, dv[2], 0.0).astype(BF16)
    d_entry = dot_nt(r.dqkv[m], wq[...])
    x = r.x[m]
    scale_one = norm_scale(x)
    n1 = x * scale_one
    r.gsum[m, 0:1, :] = jnp.sum(d_entry * n1, axis=0, keepdims=True)
    return d_middle + norm_back(d_entry * g1, n1, scale_one)


def whole(ref, cols=slice(None)):
    value = ref[:, :, cols]
    return value.reshape(M, value.shape[-1])


def store(flat, start, block):
    flat[0, start : start + OWN] = block[:OWN].astype(BF16)
    flat[1, start : start + OWN] = block[OWN:].astype(BF16)


def gate_grads(r, flat, done):
    second_t = whole(r.sec).T
    for ref, start in ((r.dg, GATE), (r.du, UP)):
        for b in range(0, 12, 2):
            g = dot(second_t, whole(ref, slice(128 * b, 128 * b + 256)))
            store(flat, start + b * OWN, g[:, :128])
            store(flat, start + (b + 1) * OWN, g[:, 128:])
            done(start + (b + 2) * OWN)


def down_grads(r, flat, done):
    df_t = whole(r.df).T
    for b in range(6):
        for owner in range(2):
            first = 768 * owner + 128 * b
            g = dot(df_t, whole(r.inn, slice(first, first + 128)))
            flat[owner, DOWN + b * D : DOWN + (b + 1) * D] = g.astype(BF16)
        done(DOWN + (b + 1) * D)


def rest_grads(r, flat, done):
    entry_t = whole(r.ent).T
    mixed_t = whole(r.mix).T
    for b in range(0, 8, 2):
        g = dot(entry_t, whole(r.dqkv, slice(128 * b, 128 * b + 256)))
        store(flat, QKV + b * OWN, g[:, :128])
        if b == 6:
            rest = whole(r.db, slice(512, 576)).astype(F32)
            rest = jnp.concatenate([rest, jnp.zeros((M, 64), F32)], axis=1)
            rest = pltpu.roll(rest, 64, 1).astype(BF16)
            store(flat, QKV + 7 * OWN, g[:, 128:] + dot(mixed_t, rest))
        else:
            store(flat, QKV + (b + 1) * OWN, g[:, 128:])
        done(QKV + (b + 2) * OWN)
    for b in range(0, 4, 2):
        g = dot(mixed_t, whole(r.db, slice(128 * b, 128 * b + 256)))
        store(flat, OUT + b * OWN, g[:, :128])
        store(flat, OUT + (b + 1) * OWN, g[:, 128:])
        done(OUT + (b + 2) * OWN)
    sums = r.gsum[0] + r.gsum[1]
    row = lax.broadcasted_iota(jnp.int32, (128, D), 0)
    store(flat, GAIN, jnp.where(row == 0, sums[0:1], jnp.where(row == 1, sums[1:2], 0.0)).T)
    flat[0, USED:] = jnp.zeros((FLAT - USED, 128), BF16)
    flat[1, USED:] = jnp.zeros((FLAT - USED, 128), BF16)
    done(FLAT)


KEPT = dict(
    wq=((D, 1024), BF16),
    wo=((D, D), BF16),
    wg=((D, FF), BF16),
    wu=((D, FF), BF16),
    wd=((D, FF), BF16),
    gains=((8, D), F32),
    x=((MICRO, ROWS, D), F32),
    dy=((MICRO, ROWS, D), F32),
    lens=((MICRO, 8, 128), F32),
    lens_own=((MICRO, 8, 128), F32),
    lens_pair=((MICRO, 8, 128), F32),
    cot_pair=((MICRO, D, ROWS), BF16),
    tok=((MICRO, D, ROWS), BF16),
    y_send=((MICRO, ROWS, D), BF16),
    y_box=((MICRO, ROWS, D), BF16),
    y_turn=((MICRO, D, ROWS), BF16),
    dx_send=((MICRO, ROWS, D), BF16),
    dx_box=((MICRO, ROWS, D), BF16),
    dx_turn=((MICRO, D, ROWS), BF16),
    ent=((MICRO, ROWS, D), BF16),
    qs=((MICRO, 3, 3 * ROWS, 128), BF16),
    kd=((MICRO, 3, ROWS, 128), BF16),
    vd=((MICRO, 3, ROWS, 128), BF16),
    pr=((MICRO, 3, 3 * ROWS, 128), F32),
    mix=((MICRO, ROWS, D), BF16),
    mid=((MICRO, ROWS, D), F32),
    sec=((MICRO, ROWS, D), BF16),
    inn=((MICRO, ROWS, FF), BF16),
    fa=((MICRO, ROWS, FF), F32),
    fb=((MICRO, ROWS, FF), F32),
    cs=((MICRO, ROWS, 128), F32),
    sn=((MICRO, ROWS, 128), F32),
    df=((MICRO, ROWS, D), BF16),
    dg=((MICRO, ROWS, FF), BF16),
    du=((MICRO, ROWS, FF), BF16),
    db=((MICRO, ROWS, D), BF16),
    dqkv=((MICRO, ROWS, 1024), BF16),
    gsum=((MICRO, 8, D), F32),
    flat=((2, FLAT, 128), BF16),
    cross=((FLAT, 128), BF16),
    one=((6 * PARTS, max(SIZE) // 8, 128), BF16),
    two=((7 * PARTS, max(SIZE) // 32, 128), BF16),
    o=((FLAT, 128), BF16),
)
SEMS = dict(
    w=7,
    swap=2,
    y=2,
    dx=2,
    y_swap=2,
    dx_swap=2,
    cross=4 * PARTS,
    one=6 * PARTS,
    two=7 * PARTS,
    along=7 * PARTS,
    back=12 * PARTS,
)


def vmem(n):
    return [pl.BlockSpec(memory_space=pltpu.VMEM)] * n


def hbm(n):
    return [pl.BlockSpec(memory_space=pl.ANY)] * n


PLANE = [(0, 1), (1, 0), (3, 0), (1, 1), (3, 1), (2, 0), (2, 1)]


def places():
    section, core, replica = (lax.axis_index(a) for a in ("section", "shard", "replica"))
    x, y, z = replica // 8, replica // 2 % 4, replica % 2

    def at(x_, y_, z_):
        return (section, core, x_ * 8 + y_ * 2 + z_)

    return SimpleNamespace(
        section=section,
        core=core,
        x=x,
        y=y,
        z=z,
        x_next=at((x + 1) % 4, y, z),
        x_prev=at((x + 3) % 4, y, z),
        y_next=at(x, (y + 1) % 4, z),
        y_prev=at(x, (y + 3) % 4, z),
        z_pair=at(x, y, 1 - z),
        x_plane=[at((x + k) % 4, y, (z + w) % 2) for k, w in PLANE],
        y_plane=[at(x, (y + k) % 4, (z + w) % 2) for k, w in PLANE],
        partner=(section, 1 - core, replica),
        across=(1 - section, core, x * 8 + y * 2 + (1 - z)),
    )


def step_kernel(
    lens, tok, cot, gain_one, gain_two, wq_own, wk_own, wv_own, wo_own, wg_own, wu_own, wd_own,
    y_out, dx_out, o, *refs
):
    r = SimpleNamespace(**dict(zip(KEPT, refs)))
    sends = dict(zip(SEMS, refs[len(KEPT) :]))
    recvs = dict(zip(SEMS, refs[len(KEPT) + len(SEMS) :]))
    local = refs[len(KEPT) + 2 * len(SEMS)]
    at = places()
    section, core = at.section, at.core

    barrier = pltpu.get_barrier_semaphore()
    near = [at.partner, at.across, *at.x_plane, *at.y_plane[1:]]
    for device in near:
        pl.semaphore_signal(barrier, inc=1, device_id=device, device_id_type=MESH)
    def remote(name, i, src, dst, device):
        return pltpu.make_async_remote_copy(
            src,
            dst,
            sends[name].at[i],
            recvs[name].at[i],
            device_id=device,
            device_id_type=MESH,
        )

    tok_load = pltpu.make_async_copy(tok, r.tok, local.at[6])

    @pl.when(section == 0)
    def _():
        tok_load.start()

    own_rows = pl.ds(pl.multiple_of(core * OWN, 16), OWN)
    own_cols = pl.ds(pl.multiple_of(core * (FF // 2), 128), FF // 2)
    weight_places = {"wo": (wo_own, r.wo.at[own_rows])}
    for j in range(0, FF, FF // 2):
        cols = slice(j, j + FF // 2)
        weight_places["wg" + str(j)] = (wg_own.at[:, cols], r.wg.at[own_rows, cols])
        weight_places["wu" + str(j)] = (wu_own.at[:, cols], r.wu.at[own_rows, cols])
    weight_places["wd"] = (wd_own, r.wd.at[:, own_cols])
    side_place = r.wq.at[own_rows]
    weight_copies = {"side": [remote("w", 0, side_place, side_place, at.partner)]}
    for i, (name, (src, dst)) in enumerate(weight_places.items()):
        weight_copies[name] = [
            remote("w", i + 1, src, dst, at.partner),
            pltpu.make_async_copy(src, dst, local.at[i]),
        ]
        weight_copies[name][1].start()
    r.wq[own_rows, :512] = wq_own[:, :512]
    for start, value in side_rows(wq_own, wk_own, wv_own, gain_one, gain_two).items():
        r.wq[own_rows, start : start + 128] = value.astype(BF16)

    r.lens_own[...] = jnp.zeros((MICRO, 8, 128), F32)
    for m in range(MICRO):
        r.lens_own[m, 0:1, 0:2] = lens[m : m + 1, :].astype(F32)
    lens_swap = remote("swap", 0, r.lens_own, r.lens_pair, at.z_pair)
    cot_swap = remote("swap", 1, cot, r.cot_pair, at.z_pair)

    pl.semaphore_wait(barrier, len(near))
    for name in ("side", "wo"):
        weight_copies[name][0].start()
    lens_swap.start()
    cot_swap.start()

    @pl.when(section == 0)
    def _():
        r.lens[...] = r.lens_own[...]
        tok_load.wait()
        for m in range(MICRO):
            r.x[m] = r.tok[m].astype(F32).T

    @pl.when(section == 1)
    def _():
        lens_swap.wait_recv()
        r.lens[...] = r.lens_pair[...]

    for m in range(MICRO):
        tables(r, m)
    weight_copies["side"][0].wait_recv()
    for name in weight_places:
        if name != "wo":
            weight_copies[name][0].start()
    r.gains[...] = r.wq[:, 896:1024].astype(F32).T[64:72]

    def y_copy(m):
        return remote("y", m, r.y_send.at[m], r.y_box.at[m], at.across)

    def dx_copy(m):
        return remote("dx", m, r.dx_send.at[m], r.dx_box.at[m], at.across)

    def y_swap(m):
        return remote("y_swap", m, r.y_turn.at[m], y_out.at[m], at.z_pair)

    def y_store(m):
        return pltpu.make_async_copy(r.y_turn.at[m], y_out.at[m], local.at[6 + m])

    def dx_store(m):
        return pltpu.make_async_copy(r.dx_turn.at[m], dx_out.at[m], local.at[8 + m])

    def dx_swap(m):
        return remote("dx_swap", m, r.dx_turn.at[m], dx_out.at[m], at.z_pair)

    total = Total(r, at, remote)

    def tick(t, carry):
        m = jnp.where(section == 0, t % 2, t // 2)
        ahead = jnp.where(section == 0, t // 2, t % 2) == 0

        @pl.when(ahead)
        def _():
            @pl.when(section == 1)
            def _():
                y_copy(m).wait_recv()
                r.x[m] = r.y_box[m].astype(F32)

            def arrived(name):
                @pl.when(t == 0)
                def _():
                    for i, copy in enumerate(weight_copies[name]):
                        if i == 0:
                            copy.wait_recv()
                        else:
                            copy.wait()

            y = forward(r, m, arrived)
            r.y_send[m] = y.astype(BF16)

            @pl.when(section == 0)
            def _():
                y_copy(m).start()
                r.y_turn[m] = r.y_send[m].astype(F32).T.astype(BF16)
                y_store(m).start()

            @pl.when(section == 1)
            def _():
                r.y_turn[m] = r.y_send[m].astype(F32).T.astype(BF16)
                y_swap(m).start()

        @pl.when(jnp.logical_not(ahead))
        def _():
            @pl.when(section == 0)
            def _():
                dx_copy(m).wait_recv()
                r.dy[m] = r.dx_box[m].astype(F32)

            @pl.when(section == 1)
            def _():
                @pl.when(t == 1)
                def _():
                    cot_swap.wait_recv()

                ids = lax.broadcasted_iota(jnp.int32, (ROWS, D), 0)
                live = ids < lengths_of(r, m)[1]
                r.dy[m] = jnp.where(live, r.cot_pair[m].astype(F32).T, 0.0)

            def halfway():
                @pl.when(jnp.logical_and(section == 0, t == 2 * MICRO - 1))
                def _():
                    gate_grads(r, r.flat, total.starter())

            r.dx_send[m] = backward(r, m, halfway).astype(BF16)

            @pl.when(section == 0)
            def _():
                r.dx_turn[m] = r.dx_send[m].astype(F32).T.astype(BF16)
                dx_store(m).start()

            @pl.when(section == 1)
            def _():
                dx_copy(m).start()
                r.dx_turn[m] = r.dx_send[m].astype(F32).T.astype(BF16)
                dx_swap(m).start()

        return carry

    lax.fori_loop(0, 2 * MICRO, tick, 0)

    @pl.when(section == 0)
    def _():
        lens_swap.wait_recv()
        cot_swap.wait_recv()

    @pl.when(section == 1)
    def _():
        gate_grads(r, r.flat, total.starter())

    started = total.starter(DOWN)
    total.step_1(0)
    down_grads(r, r.flat, started)
    rest_grads(r, r.flat, started)
    total.run(o, local)
    total.finish()

    lens_swap.wait_send()
    cot_swap.wait_send()
    for copies in weight_copies.values():
        copies[0].wait_send()

    @pl.when(section == 0)
    def _():
        for m in range(MICRO):
            y_copy(m).wait_send()
            y_store(m).wait()
            dx_store(m).wait()

    @pl.when(section == 1)
    def _():
        for m in range(MICRO):
            dx_copy(m).wait_send()
            y_swap(m).wait()
            dx_swap(m).wait()


def span(start, count):
    return pl.ds(pl.multiple_of(start, 16), count)


class Total:
    def __init__(self, r, at, remote):
        self.flat, self.box, self.one, self.two, self.o = r.flat, r.cross, r.one, r.two, r.o
        self.at, self.remote = at, remote
        self.core = at.core
        self.pos = ((at.x, at.y), (at.y, at.x))
        xs, ys = (at.x_next, at.x_prev), (at.y_next, at.y_prev)
        self.first = (xs, ys)
        self.plane = (at.y_plane, at.x_plane)
        self.sent = []
        self.copies = {}

    def send(self, name, i, src, dst, device):
        copy = self.remote(name, i, src, dst, device)
        copy.start()
        self.sent.append(copy)
        self.copies[name, i] = copy

    def got(self, name, i):
        self.copies[name, i].wait_recv()

    def cross(self, n):
        i, q = n // 4, n % 4
        count = SIZE[i] // 4
        rows = slice(BASE_ROW[i] + q * count, BASE_ROW[i] + (q + 1) * count)
        src = self.flat.at[1 - self.core, rows]
        return self.remote("cross", n, src, self.box.at[rows], self.at.partner)

    def starter(self, first=0):
        ends = [BASE_ROW[n // 4] + (n % 4 + 1) * SIZE[n // 4] // 4 for n in range(4 * PARTS)]
        begun = [sum(end <= first for end in ends)]

        def ready(rows):
            while begun[0] < len(ends) and ends[begun[0]] <= rows:
                self.cross(begun[0]).start()
                begun[0] += 1

        return ready

    def rows(self, i, k, start=0, count=None):
        place = SIZE[i] // 4 * ((self.pos[i % 2][0] + k) % 4)
        return span(BASE_ROW[i] + place + start, count)

    def piece(self, i, k):
        return SIZE[i] // 16 * ((self.pos[i % 2][1] + k) % 4)

    def add(self, i, k, upper, *others):
        count = SIZE[i] // 8
        rows = self.rows(i, k, upper * count, count)
        value = self.flat[self.core, rows].astype(F32) + self.box[rows].astype(F32)
        for other in others:
            value = value + other.astype(F32)
        self.flat[self.core, rows] = value.astype(BF16)
        return self.flat.at[self.core, rows]

    def go(self, i, slot, ref, way):
        device = self.first[i % 2][way]
        box = self.one.at[i * 6 + slot, : SIZE[i] // 8]
        self.send("one", i * 6 + slot, ref, box, device)

    def box_of(self, i, slot):
        self.got("one", i * 6 + slot)
        return self.one[i * 6 + slot, : SIZE[i] // 8]

    def step_1(self, c):
        for i in (2 * c, 2 * c + 1):
            for q in range(4):
                self.cross(i * 4 + q).wait_recv()
            self.go(i, 0, self.add(i, 2, 0), 0)
            self.go(i, 1, self.add(i, 2, 1), 1)
        for i in (2 * c, 2 * c + 1):
            self.go(i, 2, self.add(i, 1, 1), 0)
            self.go(i, 3, self.add(i, 3, 0), 1)

    def step_2(self, c):
        for i in (2 * c, 2 * c + 1):
            self.go(i, 4, self.add(i, 1, 0, self.box_of(i, 0)), 0)
            self.go(i, 5, self.add(i, 3, 1, self.box_of(i, 1)), 1)

    def block(self, i, k, w):
        count = SIZE[i] // 32
        return self.rows(i, 0, self.piece(i, k) + count * ((self.at.z + w) % 2), count)

    def two_box(self, i, j):
        return self.two.at[i * 7 + j, : SIZE[i] // 32]

    def step_3(self, c):
        for i in (2 * c, 2 * c + 1):
            self.add(i, 0, 0, self.box_of(i, 3), self.box_of(i, 4))
            self.add(i, 0, 1, self.box_of(i, 2), self.box_of(i, 5))
            for j, (k, w) in enumerate(PLANE):
                src = self.flat.at[self.core, self.block(i, k, w)]
                self.send("two", i * 7 + j, src, self.two_box(i, j), self.plane[i % 2][j])

    def step_4(self, c):
        for i in (2 * c, 2 * c + 1):
            rows = self.block(i, 0, 0)
            value = self.flat[self.core, rows].astype(F32)
            for j in range(7):
                self.got("two", i * 7 + j)
                value = value + self.two[i * 7 + j, : SIZE[i] // 32].astype(F32)
            self.o[rows] = value.astype(BF16)
            ref = self.o.at[rows]
            for j in range(7):
                self.send("along", i * 7 + j, ref, ref, self.plane[i % 2][j])

    def unit(self, i, k1, k2):
        return self.o.at[self.rows(i, k1, self.piece(i, k2), SIZE[i] // 16)]

    def step_5(self, c):
        for k in (0, 1, 3, 2):
            for i in (2 * c, 2 * c + 1):
                for j, (there, _) in enumerate(PLANE):
                    if there == k:
                        self.got("along", i * 7 + j)
                back = (4 - k) % 4
                ref = self.unit(i, 0, back)
                for d in range(2):
                    self.send("back", i * 12 + d * 6 + back, ref, ref, self.first[i % 2][d])

    def step_6(self, c):
        for k in (0, 3, 1, 2):
            for i in (2 * c, 2 * c + 1):
                way = 0 if k in (0, 3) else 1
                self.got("back", i * 12 + way * 6 + k)
                ref = self.unit(i, 1 if way else 3, k)
                slot = i * 12 + way * 6 + (4 if k < 2 else 5)
                self.send("back", slot, ref, ref, self.first[i % 2][way])

    def step_7(self, c):
        for i in (2 * c, 2 * c + 1):
            for slot in (1, 2, 6, 9, 4, 5, 10, 11):
                self.got("back", i * 12 + slot)
        rows = slice(BASE_ROW[2 * c], BASE_ROW[2 * c] + CHUNKS[c])
        copy = pltpu.make_async_copy(self.o.at[rows], self.out.at[rows], self.sem.at[c])
        copy.start()
        self.written.append(copy)

    def run(self, out, sem):
        self.out, self.sem, self.written = out, sem, []
        for n in range(2, 7 + len(CHUNKS)):
            for c in range(len(CHUNKS)):
                if 1 <= n - c <= 7:
                    getattr(self, f"step_{n - c}")(c)
        for copy in self.written:
            copy.wait()

    def finish(self):
        for n in range(4 * PARTS):
            self.cross(n).wait_send()
        for copy in self.sent:
            copy.wait_send()


def run_step(lens, tok, cot, gain_one, gain_two, wq, wk, wv, wo, wg, wu, wd):
    rows = jax.ShapeDtypeStruct((MICRO, D, ROWS), BF16)
    sems = [pltpu.SemaphoreType.DMA((n,)) for n in SEMS.values()]
    return pl.pallas_call(
        step_kernel,
        out_shape=[rows, rows, jax.ShapeDtypeStruct((FLAT, 128), BF16)],
        in_specs=vmem(1) + hbm(2) + vmem(5) + hbm(4),
        out_specs=hbm(3),
        scratch_shapes=[pltpu.VMEM(*v) for v in KEPT.values()]
        + sems
        + sems
        + [pltpu.SemaphoreType.DMA((10,))],
        compiler_params=pltpu.CompilerParams(
            collective_id=1, has_side_effects=True, vmem_limit_bytes=VMEM_LIMIT
        ),
    )(lens, tok, cot, gain_one, gain_two, wq, wk, wv, wo, wg, wu, wd)


def unpack_kernel(
    f, y, dx, y_out, dx_out, gain_one, wq, wk, wv, wo, gain_two, wg, wu, wd, *refs
):
    flat, s_y, s_dx, s_wq, s_wk, s_wv, s_wo, s_wg, s_wu, s_wd, arrive, leave = refs
    step = 6 * OWN
    bounds = (*range(0, QKV, step), QKV, USED)
    loads = []

    def load(src, dst):
        loads.append(pltpu.make_async_copy(src, dst, arrive.at[len(loads)]))
        loads[-1].start()

    for i in range(len(bounds) - 1):
        part = slice(bounds[i], bounds[i + 1])
        load(f.at[part], flat.at[part])
    load(y, s_y)
    load(dx, s_dx)
    stores = []

    def put(src, dst):
        stores.append(pltpu.make_async_copy(src, dst, leave.at[len(stores)]))
        stores[-1].start()

    def rows(start, count=OWN):
        return flat[start : start + count].astype(F32)

    n = 0
    for start, stage, dst in ((GATE, s_wg, wg), (UP, s_wu, wu)):
        for j in range(0, 12, 6):
            loads[n].wait()
            n += 1
            for b in range(j, j + 6):
                stage[:, 128 * b : 128 * b + 128] = rows(start + b * OWN)
            cols = slice(128 * j, 128 * j + 768)
            put(stage.at[:, cols], dst.at[0, :, cols])
    for j in range(0, 6, 3):
        loads[n].wait()
        n += 1
        for b in range(j, j + 3):
            s_wd[:, 128 * b : 128 * b + 128] = rows(DOWN + b * D, D)
        cols = slice(128 * j, 128 * j + 384)
        put(s_wd.at[:, cols], wd.at[0, :, cols])
    loads[n].wait()
    n += 1
    swap = [pltpu.roll(rows(QKV + b * OWN), 64, 1) for b in range(4, 8)]
    lane = lax.broadcasted_iota(jnp.int32, (OWN, 128), 1)
    for b in range(4):
        s_wq[:, 128 * b : 128 * b + 128] = rows(QKV + b * OWN)
        s_wo[:, 128 * b : 128 * b + 128] = rows(OUT + b * OWN)
    s_wq[:, 512:576] = rows(QKV + 4 * OWN)[:, :64]
    put(s_wq, wq.at[0])
    s_wo[:, 512:576] = swap[3][:, :64]
    put(s_wo, wo.at[0])
    s_wk[:, :128] = jnp.where(lane < 64, swap[0], swap[1])
    s_wk[:, 128:] = swap[1][:, :64]
    put(s_wk, wk.at[0])
    s_wv[:, :128] = rows(QKV + 6 * OWN)
    s_wv[:, 128:] = rows(QKV + 7 * OWN)[:, :64]
    put(s_wv, wv.at[0])
    for src, dst in ((s_y, y_out), (s_dx, dx_out)):
        loads[n].wait()
        n += 1
        put(src, dst)
    gains = rows(GAIN).T
    gain_one[...] = gains[0:1]
    gain_two[...] = gains[1:2]
    for copy in stores:
        copy.wait()


def run_unpack(flat, y, dx):
    kinds = [(1, OWN), (1, OWN, D), (1, OWN, 192), (1, OWN, 192), (1, OWN, D)]
    kinds += [(1, OWN), (1, OWN, FF), (1, OWN, FF), (1, D, FF // 2)]
    stages = [pltpu.VMEM(k[1:], F32) for k in kinds if len(k) == 3]
    return pl.pallas_call(
        unpack_kernel,
        out_shape=[jax.ShapeDtypeStruct(a.shape, a.dtype) for a in (y, dx)]
        + [jax.ShapeDtypeStruct(k, F32) for k in kinds],
        in_specs=hbm(3),
        out_specs=hbm(2) + [(vmem if len(k) == 2 else hbm)(1)[0] for k in kinds],
        scratch_shapes=[pltpu.VMEM((FLAT, 128), BF16)]
        + [pltpu.VMEM(y.shape, y.dtype)] * 2
        + stages
        + [pltpu.SemaphoreType.DMA((9,)), pltpu.SemaphoreType.DMA((12,))],
        compiler_params=pltpu.CompilerParams(vmem_limit_bytes=VMEM_LIMIT),
    )(flat, y, dx)


def shards(
    tokens,
    cotangent,
    seq_lengths,
    gain_attn,
    w_query,
    w_key,
    w_value,
    w_out,
    gain_ffn,
    w_gate,
    w_up,
    w_down,
):
    y, dx, flat = run_step(
        seq_lengths,
        jnp.swapaxes(tokens, 1, 2),
        jnp.swapaxes(cotangent, 1, 2),
        gain_attn,
        gain_ffn,
        w_query[0],
        w_key[0],
        w_value[0],
        w_out[0],
        w_gate[0],
        w_up[0],
        w_down[0].T,
    )
    y, dx, *grads = run_unpack(flat, y, dx)
    grads[8] = jnp.swapaxes(grads[8], 1, 2)
    return (jnp.swapaxes(y, 1, 2)[None], jnp.swapaxes(dx, 1, 2)[None], *grads)


def solution(mesh):
    row_spec = P(None, ("shard", "replica"), None)
    out_spec = P("section", None, ("shard", "replica"), None)
    vector = P("section", "shard")
    matrix = P("section", "shard", None)
    weight_specs = (vector, matrix, matrix, matrix, matrix, vector, matrix, matrix, matrix)
    return jax.shard_map(
        shards,
        mesh=mesh,
        in_specs=(row_spec, row_spec, P(None, ("shard", "replica")), *weight_specs),
        out_specs=(out_spec, out_spec, *weight_specs),
        check_vma=False,
    )
```
